128 devices in a mesh: gy: 16 (over y_lo, z, core), gx: 8 (over x, y_hi).
Axes of the slice: x: 4, y: 4 (y_hi: 2, y_lo: 2; y = y_hi * 2 + y_lo), z: 4, core: 2. Of those that a mesh axis runs over, the one named last changes fastest.
Arguments:
- tokens: bfloat16 [512, 1024, 256], P('gy', 'gx'), may hold values from -40 to 40
- cotangent: bfloat16 [512, 1024, 256], P('gy', 'gx'), may hold values from -6 to 6
- norm1_gain: float32 [256], replicated, may hold values from 0.25 to 1.75
- w_qkv: bfloat16 [256, 768], replicated, may hold values from -0.375 to 0.375
- w_out: bfloat16 [256, 256], replicated, may hold values from -0.375 to 0.375
- pos_bias: float32 [8, 64, 64], replicated, may hold values from -3.5 to 302
- norm2_gain: float32 [256], replicated, may hold values from 0.25 to 1.75
- w_up: bfloat16 [256, 1024], replicated, may hold values from -0.375 to 0.375
- w_down: bfloat16 [1024, 256], replicated, may hold values from -0.1875 to 0.1875
Outputs:
- mixed: bfloat16 [512, 1024, 256], P('gy', 'gx')
- grad_tokens: bfloat16 [512, 1024, 256], P('gy', 'gx')
- grad_qkv: float32 [256, 768], replicated
- grad_out: float32 [256, 256], replicated
The draws below stay inside these ranges and needn't reach their ends.
All inputs are finite; a program needn't handle non-finite values.
Results may differ from the reference program's by a relative error of at most 0.009.
Values may be sent and summed in bfloat16 or wider, within the bound.
No kernel may reach another device: no remote copies, remote signals or barrier semaphores. Data moves between devices by JAX's collectives and lax.ppermute only.
A program may use at most 192 MiB of HBM per device.

```python
import math
import jax
import jax.numpy as jnp
from jax import lax

C = 256
HEADS = 8
FF = 1024
GRID = 8
ROWS = 512
COLS = 1024


def draw_tokens(key, part):
    key = jax.random.fold_in(key, 11)
    base_key, row_key, chan_key = jax.random.split(key, 3)
    shape = (ROWS, COLS, C)
    base = jnp.clip(jax.random.normal(base_key, shape, jnp.float32), -4.0, 4.0)
    row_scale = jnp.exp(jax.random.uniform(row_key, (ROWS, COLS, 1), jnp.float32, math.log(0.3), math.log(3.0)))
    chan_scale = jnp.exp(jax.random.uniform(chan_key, (C,), jnp.float32, math.log(0.3), math.log(3.0)))
    return (base * row_scale * chan_scale).astype(jnp.bfloat16)


def draw_pos_bias(key, part):
    key = jax.random.fold_in(key, 23)
    keys = jax.random.split(key, 1)
    members = GRID * GRID
    shape = (HEADS, members, members)
    return jnp.clip(jax.random.normal(keys[0], shape, jnp.float32), -3.0, 3.0)


def steps_of(stream_key, shape, pieces, low, high):
    factor_of, own = 1.0, jax.random.fold_in(stream_key, 6)
    for axis_at, shards_of in pieces:
        heights = jnp.exp(jax.random.uniform(jax.random.fold_in(own, axis_at), (shards_of,), jnp.float32, low / len(pieces), high / len(pieces)))
        factor_of = factor_of * jnp.repeat(heights, shape[axis_at] // shards_of).reshape([-1 if axis == axis_at else 1 for axis in range(len(shape))])
    return factor_of


def centred(rng, dims, deviation, bound, pieces=(), held_as=jnp.bfloat16):
    array = jax.random.normal(rng, dims, jnp.float32) * deviation
    if len(pieces) > 0:
        array = steps_of(rng, dims, pieces, -0.22, 0.18) * array
    return jnp.clip(array, min=-bound, max=bound).astype(held_as)


def setup_inputs(seed: int = 0) -> dict:
    streams_of = jax.random.split(jax.random.key(seed), 10)
    return {
        "tokens": draw_tokens(jax.random.fold_in(streams_of[9], 71), 0),
        "cotangent": centred(streams_of[1], (ROWS, COLS, C), 1.0, 6.0, ((0, 16), (1, 8))),
        "norm1_gain": jnp.clip(1.0 + 0.15 * jax.random.normal(streams_of[2], (C,), jnp.float32), 0.25, 1.75),
        "w_qkv": centred(streams_of[3], (C, 3 * C), C ** -0.5, 0.375),
        "w_out": centred(streams_of[4], (C, C), C ** -0.5, 0.375),
        "pos_bias": draw_pos_bias(jax.random.fold_in(streams_of[9], 71), 0),
        "norm2_gain": jnp.clip(1.0 + 0.15 * jax.random.normal(streams_of[6], (C,), jnp.float32), 0.25, 1.75),
        "w_up": centred(streams_of[7], (C, FF), C ** -0.5, 0.375),
        "w_down": centred(streams_of[8], (FF, C), FF ** -0.5, 0.1875),
    }


EPSILON = 1e-05

def rounded(values):
    return lax.optimization_barrier(values.astype(jnp.bfloat16)).astype(jnp.float32)

def normalize(values, gain):
    wide = values.astype(jnp.float32)
    centre = lax.optimization_barrier(jnp.mean(wide, axis=-1, keepdims=True))
    shifted = wide - centre
    variance = lax.optimization_barrier(jnp.mean(shifted * shifted, axis=-1, keepdims=True))
    inverse = lax.rsqrt(variance + EPSILON)
    unit = shifted * inverse
    return (unit * gain, unit, inverse)

def feed_forward(attended, norm2_gain, w_up, w_down):
    normed_wide, unit, inverse = normalize(attended, norm2_gain)
    normed2 = normed_wide.astype(jnp.bfloat16)
    hidden = jax.nn.gelu(jnp.dot(normed2, w_up, preferred_element_type=jnp.float32)).astype(jnp.bfloat16)
    return (attended.astype(jnp.float32) + jnp.dot(hidden, w_down, preferred_element_type=jnp.float32)).astype(jnp.bfloat16)

def layer_block(x_rows, g_rows, norm1_gain, w_qkv, w_out, pos_bias, norm2_gain, w_up, w_down, groups):
    channels = x_rows.shape[-1]
    heads = pos_bias.shape[0]
    members = pos_bias.shape[1]
    width = channels // heads
    scale_factor = 1.0 / math.sqrt(width)
    normed_wide, unit, inverse = normalize(x_rows, norm1_gain)
    normed = normed_wide.astype(jnp.bfloat16)
    qkv = jnp.dot(normed, w_qkv, preferred_element_type=jnp.float32)
    split_qkv = rounded(qkv).reshape(groups, members, 3, heads, width)
    query = split_qkv[:, :, 0]
    keys = split_qkv[:, :, 1]
    values = split_qkv[:, :, 2]
    scores = jnp.einsum('nmhd,nkhd->nhmk', query, keys) * scale_factor + pos_bias[None]
    soft = jax.nn.softmax(scores, axis=-1)
    soft_low = rounded(soft)
    context = jnp.einsum('nhmk,nkhd->nmhd', soft_low, values).astype(jnp.bfloat16).reshape(groups * members, channels)
    attended = (x_rows.astype(jnp.float32) + jnp.dot(context, w_out, preferred_element_type=jnp.float32)).astype(jnp.bfloat16)
    mixed = feed_forward(attended, norm2_gain, w_up, w_down)
    d_context = jnp.dot(g_rows, w_out.T, preferred_element_type=jnp.float32).astype(jnp.bfloat16)
    d_wout = jnp.dot(context.T, g_rows, preferred_element_type=jnp.float32)
    d_ctx = d_context.astype(jnp.float32).reshape(groups, members, heads, width)
    d_soft = jnp.einsum('nmhd,nkhd->nhmk', d_ctx, values)
    d_scores = soft * (d_soft - lax.optimization_barrier(jnp.sum(soft * d_soft, axis=-1, keepdims=True)))
    d_scaled = rounded(d_scores * scale_factor)
    d_query = jnp.einsum('nhmk,nkhd->nmhd', d_scaled, keys)
    d_keys = jnp.einsum('nhmk,nmhd->nkhd', d_scaled, query)
    d_values = jnp.einsum('nhmk,nmhd->nkhd', soft_low, d_ctx)
    d_qkv = jnp.stack([d_query, d_keys, d_values], axis=2).astype(jnp.bfloat16).reshape(groups * members, 3 * channels)
    d_wqkv = jnp.dot(normed.T, d_qkv, preferred_element_type=jnp.float32)
    d_normed = jnp.dot(d_qkv, w_qkv.T, preferred_element_type=jnp.float32)
    d_unit = d_normed * norm1_gain
    d_x = inverse * (d_unit - lax.optimization_barrier(jnp.mean(d_unit, axis=-1, keepdims=True)) - unit * lax.optimization_barrier(jnp.mean(d_unit * unit, axis=-1, keepdims=True)))
    grad_rows = (g_rows.astype(jnp.float32) + d_x).astype(jnp.bfloat16)
    return (mixed, grad_rows, d_wqkv, d_wout)

def reference(tokens, cotangent, norm1_gain, w_qkv, w_out, pos_bias, norm2_gain, w_up, w_down):
    rows, cols, channels = tokens.shape
    stride_r = rows // GRID
    stride_c = cols // GRID
    members = GRID * GRID
    total = stride_r * stride_c
    block = math.gcd(total, 64)
    count = total // block

    def group(values):
        arranged = values.reshape(GRID, stride_r, GRID, stride_c, channels).transpose(1, 3, 0, 2, 4)
        return arranged.reshape(count, block * members, channels)

    def ungroup(values):
        arranged = values.reshape(stride_r, stride_c, GRID, GRID, channels).transpose(2, 0, 3, 1, 4)
        return arranged.reshape(rows, cols, channels)

    def step_block(carry, pair):
        mixed_rows, grad_rows, d_wqkv, d_wout = layer_block(pair[0], pair[1], norm1_gain, w_qkv, w_out, pos_bias, norm2_gain, w_up, w_down, block)
        return ((carry[0] + d_wqkv, carry[1] + d_wout), (mixed_rows, grad_rows))
    start = (jnp.zeros((channels, 3 * channels), jnp.float32), jnp.zeros((channels, channels), jnp.float32))
    sums, outputs = lax.scan(step_block, start, (group(tokens), group(cotangent)))
    factor = 1.0 / math.sqrt(rows * cols)
    return (ungroup(outputs[0]), ungroup(outputs[1]), sums[0] * factor, sums[1] * factor)
```

```python
import functools
import math

import jax
import jax.numpy as jnp
from jax import lax
from jax.experimental import pallas as pl
from jax.experimental.pallas import tpu as pltpu
from jax.sharding import PartitionSpec as P

GRID = 8
MEMBERS = GRID * GRID
EPSILON = 1e-05
LOG2E = math.log2(math.e)
AXES = ("gy", "gx")
LANES = 128
BLOCK = 16
BATCH = 4


def dot(a, b, contract=((1,), (0,))):
    return lax.dot_general(a, b, (contract, ((), ())), preferred_element_type=jnp.float32)


def normalize(wide, gain):
    centre = jnp.mean(wide, axis=-1, keepdims=True)
    shifted = wide - centre
    variance = jnp.mean(shifted * shifted, axis=-1, keepdims=True)
    inverse = lax.rsqrt(variance + EPSILON)
    unit = shifted * inverse
    return unit * gain, unit, inverse


def gelu(x):
    inner = x * (0.7978845608028654 + 0.035677408136300125 * (x * x))
    half = 0.5 * x
    return half + half * jnp.tanh(inner)


def pick_heads(full, lane_head, per):
    out = full[(per - 1) * MEMBERS : per * MEMBERS]
    for h in range(per - 2, -1, -1):
        out = jnp.where(lane_head == h, full[h * MEMBERS : (h + 1) * MEMBERS], out)
    return out


def kernel(
    width,
    data_ref,
    gain1_ref,
    wqkv_ref,
    wout_ref,
    bias_ref,
    gain2_ref,
    wup_ref,
    wdown_ref,
    mask_ref,
    out_ref,
    dqkv_acc_ref,
    dout_acc_ref,
    xs_ref,
    gs_ref,
    mixed_ref,
    grad_ref,
):
    channels = wout_ref.shape[0]
    halves = channels // LANES
    per = LANES // width
    tokens = MEMBERS * BLOCK
    scale = 1.0 / math.sqrt(width)

    @pl.when((pl.program_id(0) == 0) & (pl.program_id(1) == 0))
    def _():
        dqkv_acc_ref[...] = jnp.zeros_like(dqkv_acc_ref)
        dout_acc_ref[...] = jnp.zeros_like(dout_acc_ref)

    for j in range(halves):
        lanes = slice(j * LANES, (j + 1) * LANES)
        xs_ref[j] = data_ref[:, 0, :, 0, :, lanes].reshape(tokens, LANES).astype(jnp.float32)
        gs_ref[j] = data_ref[:, 0, :, 1, :, lanes].reshape(tokens, LANES).astype(jnp.float32)

    lane_head = lax.broadcasted_iota(jnp.int32, (MEMBERS, LANES), 1) // width

    def grouped(ref, rows):
        return jnp.concatenate(
            [jnp.concatenate([ref[j, r, :] for j in range(halves)], axis=1) for r in rows], axis=0
        )

    def step(i, carry):
        rows = [pl.ds(i * BATCH + g, MEMBERS, stride=BLOCK) for g in range(BATCH)]
        x = grouped(xs_ref, rows)
        cot = grouped(gs_ref, rows)
        normed_wide, unit, inverse = normalize(x, gain1_ref[...])
        normed = normed_wide.astype(jnp.bfloat16)
        cot_low = cot.astype(jnp.bfloat16)
        qkv = dot(normed, wqkv_ref[...]).astype(jnp.bfloat16)
        d_context = dot(cot_low, wout_ref[...], ((1,), (1,))).astype(jnp.bfloat16)
        mask = mask_ref[...]
        contexts, d_qkvs = [], []
        for g in range(BATCH):
            part = slice(g * MEMBERS, (g + 1) * MEMBERS)
            ctx_parts, dq_parts, dk_parts, dv_parts = [], [], [], []
            for j in range(halves):
                at = j * LANES
                q = qkv[part, at : at + LANES]
                k = qkv[part, channels + at : channels + at + LANES]
                v = qkv[part, 2 * channels + at : 2 * channels + at + LANES]
                dc = d_context[part, at : at + LANES]
                q_heads = jnp.concatenate([q] * per, axis=0) * mask
                dc_heads = jnp.concatenate([dc] * per, axis=0) * mask
                scores = dot(k, q_heads, ((1,), (1,))) * (scale * LOG2E) + bias_ref[j]
                e = jnp.exp2(scores - jnp.max(scores, axis=0, keepdims=True))
                probs = e * (1.0 / jnp.sum(e, axis=0, keepdims=True))
                probs_low = probs.astype(jnp.bfloat16)
                d_probs = dot(v, dc_heads, ((1,), (1,)))
                delta = jnp.sum(probs * d_probs, axis=0, keepdims=True)
                d_scaled = (probs * (d_probs - delta) * scale).astype(jnp.bfloat16)
                dv_parts.append(dot(probs_low, dc_heads))
                dk_parts.append(dot(d_scaled, q_heads))
                ctx_parts.append(pick_heads(dot(probs_low, v, ((0,), (0,))), lane_head, per))
                dq_parts.append(pick_heads(dot(d_scaled, k, ((0,), (0,))), lane_head, per))
            contexts.append(jnp.concatenate(ctx_parts, axis=1))
            d_qkvs.append(jnp.concatenate(dq_parts + dk_parts + dv_parts, axis=1))
        context = jnp.concatenate(contexts, axis=0).astype(jnp.bfloat16)
        d_qkv = jnp.concatenate(d_qkvs, axis=0).astype(jnp.bfloat16)
        dout_acc_ref[...] += dot(context, cot_low, ((0,), (0,)))
        dqkv_acc_ref[...] += dot(normed, d_qkv, ((0,), (0,)))
        d_unit = dot(d_qkv, wqkv_ref[...], ((1,), (1,))) * gain1_ref[...]
        grad = cot + inverse * (
            d_unit
            - jnp.mean(d_unit, axis=-1, keepdims=True)
            - unit * jnp.mean(d_unit * unit, axis=-1, keepdims=True)
        )
        attended = (x + dot(context, wout_ref[...])).astype(jnp.bfloat16).astype(jnp.float32)
        normed2 = normalize(attended, gain2_ref[...])[0].astype(jnp.bfloat16)
        hidden = gelu(dot(normed2, wup_ref[...])).astype(jnp.bfloat16)
        mixed = attended + dot(hidden, wdown_ref[...])
        for g in range(BATCH):
            part = slice(g * MEMBERS, (g + 1) * MEMBERS)
            for j in range(halves):
                lanes = slice(j * LANES, (j + 1) * LANES)
                mixed_ref[j, rows[g], :] = mixed[part, lanes]
                grad_ref[j, rows[g], :] = grad[part, lanes]
        return carry

    lax.fori_loop(0, BLOCK // BATCH, step, 0)
    shape = (GRID, GRID, BLOCK, LANES)
    for j in range(halves):
        lanes = slice(j * LANES, (j + 1) * LANES)
        out_ref[:, 0, :, 0, :, lanes] = mixed_ref[j].reshape(shape).astype(jnp.bfloat16)
        out_ref[:, 0, :, 1, :, lanes] = grad_ref[j].reshape(shape).astype(jnp.bfloat16)


def fused(data, gain1, wqkv, wout, bias, gain2, wup, wdown, mask, width):
    _, classes, _, _, positions, channels = data.shape
    halves = channels // LANES
    tokens = MEMBERS * BLOCK
    whole = lambda a: pl.BlockSpec(a.shape, lambda c, p: (0,) * a.ndim)
    block = pl.BlockSpec((GRID, 1, GRID, 2, BLOCK, channels), lambda c, p: (0, c, 0, 0, p, 0))
    count = classes * positions * MEMBERS
    weights = (gain1, wqkv, wout, bias, gain2, wup, wdown, mask)
    ff = wup.shape[1]
    return pl.pallas_call(
        functools.partial(kernel, width),
        grid=(classes, positions // BLOCK),
        in_specs=[block] + [whole(a) for a in weights],
        out_specs=[
            block,
            pl.BlockSpec((channels, 3 * channels), lambda c, p: (0, 0)),
            pl.BlockSpec((channels, channels), lambda c, p: (0, 0)),
        ],
        out_shape=[
            jax.ShapeDtypeStruct(data.shape, jnp.bfloat16),
            jax.ShapeDtypeStruct((channels, 3 * channels), jnp.float32),
            jax.ShapeDtypeStruct((channels, channels), jnp.float32),
        ],
        scratch_shapes=[pltpu.VMEM((halves, tokens, LANES), jnp.float32)] * 4,
        compiler_params=pltpu.CompilerParams(vmem_limit_bytes=40 * 1024 * 1024),
        cost_estimate=pl.CostEstimate(
            flops=count * 2 * channels * (12 * channels + 2 * ff),
            bytes_accessed=2 * 2 * data.size,
            transcendentals=count * ff,
        ),
    )(data, *weights)


def prepared(gain1, gain2, pos_bias, channels):
    heads, members, _ = pos_bias.shape
    width = channels // heads
    per = LANES // width
    halves = channels // LANES
    bias = (pos_bias * LOG2E).transpose(2, 0, 1).reshape(members, halves, per * members)
    bias = bias.transpose(1, 0, 2)
    row_head = lax.broadcasted_iota(jnp.int32, (per * members, LANES), 0) // members
    lane_head = lax.broadcasted_iota(jnp.int32, (per * members, LANES), 1) // width
    mask = (row_head == lane_head).astype(jnp.bfloat16)
    return gain1.reshape(1, -1), gain2.reshape(1, -1), bias, mask, width


def reduce_everywhere(partial):
    devices = lax.axis_size(AXES)
    rows, columns = partial.shape
    pieces = partial.astype(jnp.bfloat16).reshape(devices, rows // devices, columns)
    pieces = lax.all_to_all(pieces, AXES, 0, 0, tiled=True)
    total = jnp.sum(pieces.astype(jnp.float32), axis=0).astype(jnp.bfloat16)
    spread = jnp.broadcast_to(total[None], pieces.shape)
    return lax.all_to_all(spread, AXES, 0, 0, tiled=True).astype(jnp.float32).reshape(rows, columns)


def local(tokens, cotangent, norm1_gain, w_qkv, w_out, pos_bias, norm2_gain, w_up, w_down):
    tile_rows, tile_cols, channels = tokens.shape
    row_devices = lax.axis_size("gy")
    column_devices = lax.axis_size("gx")
    devices = row_devices * column_devices
    classes = row_devices // GRID
    positions = tile_rows * tile_cols // devices
    factor = 1.0 / math.sqrt(tile_rows * tile_cols * devices)
    gain1, gain2, bias, mask, width = prepared(norm1_gain, norm2_gain, pos_bias, channels)

    sent = jnp.stack(
        [
            tokens.reshape(devices, positions, channels),
            cotangent.reshape(devices, positions, channels),
        ],
        axis=1,
    )
    data = lax.all_to_all(sent, AXES, 0, 0, tiled=True)
    data = data.reshape(GRID, classes, GRID, 2, positions, channels)
    out, d_wqkv, d_wout = fused(
        data, gain1, w_qkv, w_out, bias, gain2, w_up, w_down, mask, width
    )
    back = lax.all_to_all(
        out.reshape(devices, 2, positions, channels), AXES, 0, 0, tiled=True
    )
    mixed = back[:, 0].reshape(tokens.shape)
    grad_tokens = back[:, 1].reshape(tokens.shape)
    partial = jnp.concatenate([d_wqkv.reshape(-1, channels), d_wout], axis=0)
    total = reduce_everywhere(partial) * factor
    grad_qkv = total[: 3 * channels].reshape(channels, 3 * channels)
    return (mixed, grad_tokens, grad_qkv, total[3 * channels :])


def solution(mesh):
    placed = (P("gy", "gx", None), P("gy", "gx", None), P(), P(), P(), P(), P(), P(), P())
    return jax.shard_map(
        local,
        mesh=mesh,
        in_specs=placed,
        out_specs=(P("gy", "gx", None), P("gy", "gx", None), P(), P()),
        check_vma=False,
    )
```

```python
import functools
import math

import jax
import jax.numpy as jnp
from jax import lax
from jax.experimental import pallas as pl
from jax.experimental.pallas import tpu as pltpu
from jax.sharding import PartitionSpec as P

GRID = 8
MEMBERS = GRID * GRID
EPSILON = 1e-05
LOG2E = math.log2(math.e)
AXES = ("gy", "gx")
LANES = 128
BLOCK = 16
BATCH = 4
VMEM_LIMIT = 60 * 1024 * 1024


def dot(a, b, contract=((1,), (0,))):
    return lax.dot_general(a, b, (contract, ((), ())), preferred_element_type=jnp.float32)


def normalize(wide, gain):
    centre = jnp.mean(wide, axis=-1, keepdims=True)
    shifted = wide - centre
    variance = jnp.mean(shifted * shifted, axis=-1, keepdims=True)
    inverse = lax.rsqrt(variance + EPSILON)
    unit = shifted * inverse
    return unit * gain, unit, inverse


def gelu(x):
    inner = x * (0.7978845608028654 + 0.035677408136300125 * (x * x))
    half = 0.5 * x
    return half + half * jnp.tanh(inner)


def pick_heads(full, lane_head, per):
    out = full[(per - 1) * MEMBERS : per * MEMBERS]
    for h in range(per - 2, -1, -1):
        out = jnp.where(lane_head == h, full[h * MEMBERS : (h + 1) * MEMBERS], out)
    return out


def load_tokens(scratch_ref, data_ref):
    halves, tokens, _ = scratch_ref.shape
    for j in range(halves):
        lanes = slice(j * LANES, (j + 1) * LANES)
        scratch_ref[j] = data_ref[:, 0, :, :, lanes].reshape(tokens, LANES).astype(jnp.float32)


def store_tokens(data_ref, scratch_ref):
    halves = scratch_ref.shape[0]
    for j in range(halves):
        lanes = slice(j * LANES, (j + 1) * LANES)
        wide = scratch_ref[j].reshape(GRID, GRID, BLOCK, LANES)
        data_ref[:, 0, :, :, lanes] = wide.astype(jnp.bfloat16)


def group_rows(i):
    return [pl.ds(i * BATCH + g, MEMBERS, stride=BLOCK) for g in range(BATCH)]


def gather_groups(ref, rows):
    halves = ref.shape[0]
    return jnp.concatenate(
        [jnp.concatenate([ref[j, r, :] for j in range(halves)], axis=1) for r in rows], axis=0
    )


def scatter_groups(ref, rows, values):
    for g, r in enumerate(rows):
        for j in range(ref.shape[0]):
            ref[j, r, :] = values[g * MEMBERS : (g + 1) * MEMBERS, j * LANES : (j + 1) * LANES]


def forward_kernel(
    width,
    data_ref,
    gain1_ref,
    wqkv_ref,
    wout_ref,
    bias_ref,
    gain2_ref,
    wup_ref,
    wdown_ref,
    mask_ref,
    out_ref,
    qkv_ref,
    probs_ref,
    context_ref,
    xs_ref,
    mixed_ref,
):
    channels = wout_ref.shape[0]
    halves = channels // LANES
    per = LANES // width
    scale = 1.0 / math.sqrt(width)
    count = BATCH * MEMBERS
    load_tokens(xs_ref, data_ref)
    lane_head = lax.broadcasted_iota(jnp.int32, (MEMBERS, LANES), 1) // width

    def step(i, carry):
        rows = group_rows(i)
        here = pl.ds(pl.multiple_of(i * count, count), count)
        x = gather_groups(xs_ref, rows)
        normed = normalize(x, gain1_ref[...])[0].astype(jnp.bfloat16)
        qkv = dot(normed, wqkv_ref[...]).astype(jnp.bfloat16)
        qkv_ref[here, :] = qkv
        mask = mask_ref[...]
        contexts = []
        for g in range(BATCH):
            part = slice(g * MEMBERS, (g + 1) * MEMBERS)
            ctx_parts = []
            for j in range(halves):
                at = j * LANES
                q = qkv[part, at : at + LANES]
                k = qkv[part, channels + at : channels + at + LANES]
                v = qkv[part, 2 * channels + at : 2 * channels + at + LANES]
                q_heads = jnp.concatenate([q] * per, axis=0) * mask
                scores = dot(k, q_heads, ((1,), (1,))) * (scale * LOG2E) + bias_ref[j]
                e = jnp.exp2(scores - jnp.max(scores, axis=0, keepdims=True))
                probs = (e * (1.0 / jnp.sum(e, axis=0, keepdims=True))).astype(jnp.bfloat16)
                slot = (i * BATCH + g) * halves + j
                probs_ref[pl.ds(pl.multiple_of(slot * MEMBERS, MEMBERS), MEMBERS), :] = probs
                ctx_parts.append(pick_heads(dot(probs, v, ((0,), (0,))), lane_head, per))
            contexts.append(jnp.concatenate(ctx_parts, axis=1))
        context = jnp.concatenate(contexts, axis=0).astype(jnp.bfloat16)
        context_ref[here, :] = context
        attended = (x + dot(context, wout_ref[...])).astype(jnp.bfloat16).astype(jnp.float32)
        normed2 = normalize(attended, gain2_ref[...])[0].astype(jnp.bfloat16)
        hidden = gelu(dot(normed2, wup_ref[...])).astype(jnp.bfloat16)
        scatter_groups(mixed_ref, rows, attended + dot(hidden, wdown_ref[...]))
        return carry

    lax.fori_loop(0, BLOCK // BATCH, step, 0)
    store_tokens(out_ref, mixed_ref)


def backward_kernel(
    width,
    data_ref,
    cot_ref,
    qkv_ref,
    probs_ref,
    context_ref,
    gain1_ref,
    wqkv_ref,
    wout_ref,
    mask_ref,
    out_ref,
    dqkv_acc_ref,
    dout_acc_ref,
    xs_ref,
    gs_ref,
    grad_ref,
):
    channels = wout_ref.shape[0]
    halves = channels // LANES
    per = LANES // width
    scale = 1.0 / math.sqrt(width)
    count = BATCH * MEMBERS

    @pl.when((pl.program_id(0) == 0) & (pl.program_id(1) == 0))
    def _():
        dqkv_acc_ref[...] = jnp.zeros_like(dqkv_acc_ref)
        dout_acc_ref[...] = jnp.zeros_like(dout_acc_ref)

    load_tokens(xs_ref, data_ref)
    load_tokens(gs_ref, cot_ref)
    lane_head = lax.broadcasted_iota(jnp.int32, (MEMBERS, LANES), 1) // width

    def step(i, carry):
        rows = group_rows(i)
        here = pl.ds(pl.multiple_of(i * count, count), count)
        cot = gather_groups(gs_ref, rows)
        cot_low = cot.astype(jnp.bfloat16)
        d_context = dot(cot_low, wout_ref[...], ((1,), (1,))).astype(jnp.bfloat16)
        qkv = qkv_ref[here, :]
        mask = mask_ref[...]
        d_qkvs = []
        for g in range(BATCH):
            part = slice(g * MEMBERS, (g + 1) * MEMBERS)
            dq_parts, dk_parts, dv_parts = [], [], []
            for j in range(halves):
                at = j * LANES
                q = qkv[part, at : at + LANES]
                k = qkv[part, channels + at : channels + at + LANES]
                v = qkv[part, 2 * channels + at : 2 * channels + at + LANES]
                dc = d_context[part, at : at + LANES]
                q_heads = jnp.concatenate([q] * per, axis=0) * mask
                dc_heads = jnp.concatenate([dc] * per, axis=0) * mask
                slot = (i * BATCH + g) * halves + j
                probs_low = probs_ref[pl.ds(pl.multiple_of(slot * MEMBERS, MEMBERS), MEMBERS), :]
                probs = probs_low.astype(jnp.float32)
                d_probs = dot(v, dc_heads, ((1,), (1,)))
                delta = jnp.sum(probs * d_probs, axis=0, keepdims=True)
                d_scaled = (probs * (d_probs - delta) * scale).astype(jnp.bfloat16)
                dv_parts.append(dot(probs_low, dc_heads))
                dk_parts.append(dot(d_scaled, q_heads))
                dq_parts.append(pick_heads(dot(d_scaled, k, ((0,), (0,))), lane_head, per))
            d_qkvs.append(jnp.concatenate(dq_parts + dk_parts + dv_parts, axis=1))
        d_qkv = jnp.concatenate(d_qkvs, axis=0).astype(jnp.bfloat16)
        x = gather_groups(xs_ref, rows)
        normed_wide, unit, inverse = normalize(x, gain1_ref[...])
        dout_acc_ref[...] += dot(context_ref[here, :], cot_low, ((0,), (0,)))
        dqkv_acc_ref[...] += dot(normed_wide.astype(jnp.bfloat16), d_qkv, ((0,), (0,)))
        d_unit = dot(d_qkv, wqkv_ref[...], ((1,), (1,))) * gain1_ref[...]
        grad = cot + inverse * (
            d_unit
            - jnp.mean(d_unit, axis=-1, keepdims=True)
            - unit * jnp.mean(d_unit * unit, axis=-1, keepdims=True)
        )
        scatter_groups(grad_ref, rows, grad)
        return carry

    lax.fori_loop(0, BLOCK // BATCH, step, 0)
    store_tokens(out_ref, grad_ref)


def specs(data):
    _, classes, _, positions, channels = data.shape
    steps = positions // BLOCK
    grid = (classes, steps)
    block = pl.BlockSpec((GRID, 1, GRID, BLOCK, channels), lambda c, p: (0, c, 0, p, 0))
    whole = lambda a: pl.BlockSpec(a.shape, lambda c, p: (0,) * a.ndim)
    flat = lambda rows, width: pl.BlockSpec((rows, width), lambda c, p: (c * steps + p, 0))
    return grid, block, whole, flat, classes * positions


PARAMS = pltpu.CompilerParams(vmem_limit_bytes=VMEM_LIMIT)


def forward(data, gain1, wqkv, wout, bias, gain2, wup, wdown, mask, width):
    grid, block, whole, flat, groups = specs(data)
    channels = data.shape[-1]
    halves = channels // LANES
    tokens = MEMBERS * BLOCK
    count = groups * MEMBERS
    ff = wup.shape[1]
    row_width = mask.shape[0]
    weights = (gain1, wqkv, wout, bias, gain2, wup, wdown, mask)
    return pl.pallas_call(
        functools.partial(forward_kernel, width),
        grid=grid,
        in_specs=[block] + [whole(a) for a in weights],
        out_specs=[
            block,
            flat(tokens, 3 * channels),
            flat(tokens * halves, row_width),
            flat(tokens, channels),
        ],
        out_shape=[
            jax.ShapeDtypeStruct(data.shape, jnp.bfloat16),
            jax.ShapeDtypeStruct((count, 3 * channels), jnp.bfloat16),
            jax.ShapeDtypeStruct((count * halves, row_width), jnp.bfloat16),
            jax.ShapeDtypeStruct((count, channels), jnp.bfloat16),
        ],
        scratch_shapes=[pltpu.VMEM((halves, tokens, LANES), jnp.float32)] * 2,
        compiler_params=PARAMS,
        cost_estimate=pl.CostEstimate(
            flops=count * 2 * channels * (16 * channels + 2 * ff),
            bytes_accessed=2 * count * channels * 8,
            transcendentals=count * ff,
        ),
    )(data, *weights)


def backward(data, cot, qkv, probs, context, gain1, wqkv, wout, mask, width):
    grid, block, whole, flat, groups = specs(data)
    channels = data.shape[-1]
    halves = channels // LANES
    tokens = MEMBERS * BLOCK
    count = groups * MEMBERS
    weights = (gain1, wqkv, wout, mask)
    return pl.pallas_call(
        functools.partial(backward_kernel, width),
        grid=grid,
        in_specs=[
            block,
            block,
            flat(tokens, 3 * channels),
            flat(tokens * halves, mask.shape[0]),
            flat(tokens, channels),
        ]
        + [whole(a) for a in weights],
        out_specs=[
            block,
            pl.BlockSpec((channels, 3 * channels), lambda c, p: (0, 0)),
            pl.BlockSpec((channels, channels), lambda c, p: (0, 0)),
        ],
        out_shape=[
            jax.ShapeDtypeStruct(data.shape, jnp.bfloat16),
            jax.ShapeDtypeStruct((channels, 3 * channels), jnp.float32),
            jax.ShapeDtypeStruct((channels, channels), jnp.float32),
        ],
        scratch_shapes=[pltpu.VMEM((halves, tokens, LANES), jnp.float32)] * 3,
        compiler_params=PARAMS,
        cost_estimate=pl.CostEstimate(
            flops=count * 2 * channels * 24 * channels,
            bytes_accessed=2 * count * channels * 10,
            transcendentals=0,
        ),
    )(data, cot, qkv, probs, context, *weights)


def run_kernel(data, gain1, wqkv, wout, pos_bias, gain2, wup, wdown):
    gain1, gain2, bias, mask, width = prepared(gain1, gain2, pos_bias, data.shape[-1])
    tokens, cot = data[:, :, :, 0], data[:, :, :, 1]
    mixed, qkv, probs, context = forward(
        tokens, gain1, wqkv, wout, bias, gain2, wup, wdown, mask, width
    )
    grad, a, b = backward(tokens, cot, qkv, probs, context, gain1, wqkv, wout, mask, width)
    return jnp.stack([mixed, grad], axis=3), a, b


def prepared(gain1, gain2, pos_bias, channels):
    heads, members, _ = pos_bias.shape
    width = channels // heads
    per = LANES // width
    halves = channels // LANES
    bias = (pos_bias * LOG2E).transpose(2, 0, 1).reshape(members, halves, per * members)
    bias = bias.transpose(1, 0, 2)
    row_head = lax.broadcasted_iota(jnp.int32, (per * members, LANES), 0) // members
    lane_head = lax.broadcasted_iota(jnp.int32, (per * members, LANES), 1) // width
    mask = (row_head == lane_head).astype(jnp.bfloat16)
    return gain1.reshape(1, -1), gain2.reshape(1, -1), bias, mask, width


def exchange(pieces):
    return lax.all_to_all(pieces, AXES, 0, 0, tiled=True)


def local(tokens, cotangent, norm1_gain, w_qkv, w_out, pos_bias, norm2_gain, w_up, w_down):
    tile_rows, tile_cols, channels = tokens.shape
    devices = lax.axis_size(AXES)
    classes = lax.axis_size("gy") // GRID
    positions = tile_rows * tile_cols // devices
    factor = 1.0 / math.sqrt(tile_rows * tile_cols * devices)
    gain1, gain2, bias, mask, width = prepared(norm1_gain, norm2_gain, pos_bias, channels)
    sent = (devices, positions, channels)
    kept = (GRID, classes, GRID, positions, channels)

    data = exchange(tokens.reshape(sent)).reshape(kept)
    cot = exchange(cotangent.reshape(sent)).reshape(kept)
    mixed, qkv, probs, context = forward(
        data, gain1, w_qkv, w_out, bias, gain2, w_up, w_down, mask, width
    )
    mixed = exchange(mixed.reshape(sent))
    grad, d_wqkv, d_wout = backward(
        data, cot, qkv, probs, context, gain1, w_qkv, w_out, mask, width
    )
    partial = jnp.concatenate([d_wqkv.reshape(-1, channels), d_wout], axis=0)
    pieces = partial.astype(jnp.bfloat16).reshape(devices, -1, channels)
    joined = jnp.concatenate([grad.reshape(sent), pieces], axis=1)
    joined, mixed = lax.optimization_barrier((joined, mixed))
    joined = exchange(joined)
    total = jnp.sum(joined[:, positions:].astype(jnp.float32), axis=0) * factor
    total = total.astype(jnp.bfloat16)
    total = exchange(jnp.broadcast_to(total[None], pieces.shape)).astype(jnp.float32)
    total = total.reshape(-1, channels)
    grad_qkv = total[: 3 * channels].reshape(channels, 3 * channels)
    grad_tokens = joined[:, :positions].reshape(tokens.shape)
    return (mixed.reshape(tokens.shape), grad_tokens, grad_qkv, total[3 * channels :])


def solution(mesh):
    placed = (P("gy", "gx", None), P("gy", "gx", None), P(), P(), P(), P(), P(), P(), P())
    return jax.shard_map(
        local,
        mesh=mesh,
        in_specs=placed,
        out_specs=(P("gy", "gx", None), P("gy", "gx", None), P(), P()),
        check_vma=False,
    )
```

```python
import functools
import math

import jax
import jax.numpy as jnp
from jax import lax
from jax.experimental import pallas as pl
from jax.experimental.pallas import tpu as pltpu
from jax.sharding import PartitionSpec as P

GRID = 8
MEMBERS = GRID * GRID
EPSILON = 1e-05
LOG2E = math.log2(math.e)
AXES = ("gy", "gx")
LANES = 128
BLOCK = 16
DENSE = 16
UNROLL = 16
VMEM_LIMIT = 62 * 1024 * 1024 + 512 * 1024


def dot(a, b, contract=((1,), (0,))):
    return lax.dot_general(a, b, (contract, ((), ())), preferred_element_type=jnp.float32)


def normalize(wide, gain):
    centre = jnp.mean(wide, axis=-1, keepdims=True)
    shifted = wide - centre
    variance = jnp.mean(shifted * shifted, axis=-1, keepdims=True)
    inverse = lax.rsqrt(variance + EPSILON)
    unit = shifted * inverse
    return unit * gain, unit, inverse


def gelu(x):
    inner = x * (0.7978845608028654 + 0.035677408136300125 * (x * x))
    half = 0.5 * x
    return half + half * jnp.tanh(inner)


def pick_heads(full, lane_head, per):
    out = full[(per - 1) * MEMBERS : per * MEMBERS]
    for h in range(per - 2, -1, -1):
        out = jnp.where(lane_head == h, full[h * MEMBERS : (h + 1) * MEMBERS], out)
    return out


def load_tokens(scratch_ref, data_ref):
    halves, tokens, _ = scratch_ref.shape
    for j in range(halves):
        lanes = slice(j * LANES, (j + 1) * LANES)
        scratch_ref[j] = data_ref[:, 0, :, :, lanes].reshape(tokens, LANES).astype(jnp.float32)


def store_tokens(data_ref, scratch_ref):
    halves = scratch_ref.shape[0]
    for j in range(halves):
        lanes = slice(j * LANES, (j + 1) * LANES)
        wide = scratch_ref[j].reshape(GRID, GRID, BLOCK, LANES)
        data_ref[:, 0, :, :, lanes] = wide.astype(jnp.bfloat16)


def group_rows(i):
    return [pl.ds(i * DENSE + g, MEMBERS, stride=BLOCK) for g in range(DENSE)]


def token_rows(i):
    count = DENSE * MEMBERS
    return pl.ds(pl.multiple_of(i * count, count), count)


def gather_groups(ref, rows):
    halves = ref.shape[0]
    return jnp.concatenate(
        [jnp.concatenate([ref[j, r, :] for j in range(halves)], axis=1) for r in rows], axis=0
    )


def scatter_groups(ref, rows, values):
    for g, r in enumerate(rows):
        for j in range(ref.shape[0]):
            ref[j, r, :] = values[g * MEMBERS : (g + 1) * MEMBERS, j * LANES : (j + 1) * LANES]


def repeat(count, step):
    def body(i, carry):
        step(i)
        return carry

    lax.fori_loop(0, count, body, 0)


def forward_kernel(
    width,
    data_ref,
    gain1_ref,
    wqkv_ref,
    wout_ref,
    bias_ref,
    gain2_ref,
    wup_ref,
    wdown_ref,
    mask_ref,
    out_ref,
    qkv_ref,
    probs_ref,
    context_ref,
    xs_ref,
    mixed_ref,
):
    channels = wout_ref.shape[0]
    halves = channels // LANES
    per = LANES // width
    scale = 1.0 / math.sqrt(width)
    load_tokens(xs_ref, data_ref)
    lane_head = lax.broadcasted_iota(jnp.int32, (MEMBERS, LANES), 1) // width

    def project(i):
        x = gather_groups(xs_ref, group_rows(i))
        normed = normalize(x, gain1_ref[...])[0].astype(jnp.bfloat16)
        qkv_ref[token_rows(i), :] = dot(normed, wqkv_ref[...]).astype(jnp.bfloat16)

    def attend(i):
        units = []
        for g in range(UNROLL):
            part = pl.ds(pl.multiple_of((i * UNROLL + g) * MEMBERS, MEMBERS), MEMBERS)
            for j in range(halves):
                slot = (i * UNROLL + g) * halves + j
                units.append((part, j * LANES, j, pl.ds(pl.multiple_of(slot * MEMBERS, MEMBERS), MEMBERS)))
        scores, probs = [], []
        for part, at, j, slot in units:
            q = qkv_ref[part, at : at + LANES]
            k = qkv_ref[part, channels + at : channels + at + LANES]
            q_heads = jnp.concatenate([q] * per, axis=0) * mask_ref[...]
            scores.append(dot(k, q_heads, ((1,), (1,))))
        for (part, at, j, slot), raw in zip(units, scores):
            raw = raw * (scale * LOG2E) + bias_ref[j]
            e = jnp.exp2(raw - jnp.max(raw, axis=0, keepdims=True))
            low = (e * (1.0 / jnp.sum(e, axis=0, keepdims=True))).astype(jnp.bfloat16)
            probs_ref[slot, :] = low
            probs.append(low)
        for (part, at, j, slot), low in zip(units, probs):
            v = qkv_ref[part, 2 * channels + at : 2 * channels + at + LANES]
            context = pick_heads(dot(low, v, ((0,), (0,))), lane_head, per)
            context_ref[part, at : at + LANES] = context.astype(jnp.bfloat16)

    def finish(i):
        rows = group_rows(i)
        x = gather_groups(xs_ref, rows)
        context = context_ref[token_rows(i), :]
        attended = (x + dot(context, wout_ref[...])).astype(jnp.bfloat16).astype(jnp.float32)
        normed2 = normalize(attended, gain2_ref[...])[0].astype(jnp.bfloat16)
        hidden = gelu(dot(normed2, wup_ref[...])).astype(jnp.bfloat16)
        scatter_groups(mixed_ref, rows, attended + dot(hidden, wdown_ref[...]))

    repeat(BLOCK // DENSE, project)
    repeat(BLOCK // UNROLL, attend)
    repeat(BLOCK // DENSE, finish)
    store_tokens(out_ref, mixed_ref)


def backward_kernel(
    width,
    data_ref,
    cot_ref,
    qkv_ref,
    probs_ref,
    context_ref,
    gain1_ref,
    wqkv_ref,
    wout_ref,
    mask_ref,
    out_ref,
    partial_ref,
    acc_ref,
    xs_ref,
    gs_ref,
    grad_ref,
    dctx_ref,
    dqkv_ref,
):
    channels = wout_ref.shape[0]
    halves = channels // LANES
    per = LANES // width
    scale = 1.0 / math.sqrt(width)

    @pl.when((pl.program_id(0) == 0) & (pl.program_id(1) == 0))
    def _():
        acc_ref[...] = jnp.zeros_like(acc_ref)

    load_tokens(xs_ref, data_ref)
    load_tokens(gs_ref, cot_ref)
    lane_head = lax.broadcasted_iota(jnp.int32, (MEMBERS, LANES), 1) // width

    def project(i):
        here = token_rows(i)
        cot = gather_groups(gs_ref, group_rows(i)).astype(jnp.bfloat16)
        dctx_ref[here, :] = dot(cot, wout_ref[...], ((1,), (1,))).astype(jnp.bfloat16)
        acc_ref[3] += dot(context_ref[here, :], cot, ((0,), (0,)))

    def attend(i):
        units = []
        for g in range(UNROLL):
            part = pl.ds(pl.multiple_of((i * UNROLL + g) * MEMBERS, MEMBERS), MEMBERS)
            for j in range(halves):
                slot = (i * UNROLL + g) * halves + j
                units.append((part, j * LANES, pl.ds(pl.multiple_of(slot * MEMBERS, MEMBERS), MEMBERS)))

        def put(n, part, at, value):
            to = n * channels + at
            dqkv_ref[part, to : to + LANES] = value.astype(jnp.bfloat16)

        d_probs, d_scaled = [], []
        for part, at, slot in units:
            v = qkv_ref[part, 2 * channels + at : 2 * channels + at + LANES]
            dc_heads = jnp.concatenate([dctx_ref[part, at : at + LANES]] * per, axis=0) * mask_ref[...]
            d_probs.append(dot(v, dc_heads, ((1,), (1,))))
            put(2, part, at, dot(probs_ref[slot, :], dc_heads))
        for (part, at, slot), dp in zip(units, d_probs):
            probs = probs_ref[slot, :].astype(jnp.float32)
            delta = jnp.sum(probs * dp, axis=0, keepdims=True)
            d_scaled.append((probs * (dp - delta) * scale).astype(jnp.bfloat16))
        for (part, at, slot), ds in zip(units, d_scaled):
            q_heads = jnp.concatenate([qkv_ref[part, at : at + LANES]] * per, axis=0) * mask_ref[...]
            put(1, part, at, dot(ds, q_heads))
            k = qkv_ref[part, channels + at : channels + at + LANES]
            put(0, part, at, pick_heads(dot(ds, k, ((0,), (0,))), lane_head, per))

    def finish(i):
        rows = group_rows(i)
        x = gather_groups(xs_ref, rows)
        d_qkv = dqkv_ref[token_rows(i), :]
        normed_wide, unit, inverse = normalize(x, gain1_ref[...])
        d_weight = dot(normed_wide.astype(jnp.bfloat16), d_qkv, ((0,), (0,)))
        for n in range(3):
            acc_ref[n] += d_weight[:, n * channels : (n + 1) * channels]
        d_unit = dot(d_qkv, wqkv_ref[...], ((1,), (1,))) * gain1_ref[...]
        grad = gather_groups(gs_ref, rows) + inverse * (
            d_unit
            - jnp.mean(d_unit, axis=-1, keepdims=True)
            - unit * jnp.mean(d_unit * unit, axis=-1, keepdims=True)
        )
        scatter_groups(grad_ref, rows, grad)

    repeat(BLOCK // DENSE, project)
    repeat(BLOCK // UNROLL, attend)
    repeat(BLOCK // DENSE, finish)
    store_tokens(out_ref, grad_ref)

    last = (pl.program_id(0) == pl.num_programs(0) - 1) & (
        pl.program_id(1) == pl.num_programs(1) - 1
    )

    @pl.when(last)
    def _():
        partial_ref[...] = acc_ref[...].reshape(partial_ref.shape).astype(jnp.bfloat16)


def specs(data):
    _, classes, _, positions, channels = data.shape
    steps = positions // BLOCK
    grid = (classes, steps)
    block = pl.BlockSpec((GRID, 1, GRID, BLOCK, channels), lambda c, p: (0, c, 0, p, 0))
    whole = lambda a: pl.BlockSpec(a.shape, lambda c, p: (0,) * a.ndim)
    flat = lambda rows, width: pl.BlockSpec((rows, width), lambda c, p: (c * steps + p, 0))
    return grid, block, whole, flat, classes * positions


PARAMS = pltpu.CompilerParams(vmem_limit_bytes=VMEM_LIMIT)


def forward(data, gain1, wqkv, wout, bias, gain2, wup, wdown, mask, width):
    grid, block, whole, flat, groups = specs(data)
    channels = data.shape[-1]
    halves = channels // LANES
    tokens = MEMBERS * BLOCK
    count = groups * MEMBERS
    ff = wup.shape[1]
    row_width = mask.shape[0]
    weights = (gain1, wqkv, wout, bias, gain2, wup, wdown, mask)
    return pl.pallas_call(
        functools.partial(forward_kernel, width),
        grid=grid,
        in_specs=[block] + [whole(a) for a in weights],
        out_specs=[
            block,
            flat(tokens, 3 * channels),
            flat(tokens * halves, row_width),
            flat(tokens, channels),
        ],
        out_shape=[
            jax.ShapeDtypeStruct(data.shape, jnp.bfloat16),
            jax.ShapeDtypeStruct((count, 3 * channels), jnp.bfloat16),
            jax.ShapeDtypeStruct((count * halves, row_width), jnp.bfloat16),
            jax.ShapeDtypeStruct((count, channels), jnp.bfloat16),
        ],
        scratch_shapes=[pltpu.VMEM((halves, tokens, LANES), jnp.float32)] * 2,
        compiler_params=PARAMS,
        cost_estimate=pl.CostEstimate(
            flops=count * 2 * channels * (16 * channels + 2 * ff),
            bytes_accessed=2 * count * channels * 8,
            transcendentals=count * ff,
        ),
    )(data, *weights)


def backward(data, cot, qkv, probs, context, gain1, wqkv, wout, mask, width):
    grid, block, whole, flat, groups = specs(data)
    channels = data.shape[-1]
    halves = channels // LANES
    tokens = MEMBERS * BLOCK
    count = groups * MEMBERS
    weights = (gain1, wqkv, wout, mask)
    return pl.pallas_call(
        functools.partial(backward_kernel, width),
        grid=grid,
        in_specs=[
            block,
            block,
            flat(tokens, 3 * channels),
            flat(tokens * halves, mask.shape[0]),
            flat(tokens, channels),
        ]
        + [whole(a) for a in weights],
        out_specs=[
            block,
            pl.BlockSpec((4 * channels, channels), lambda c, p: (0, 0)),
        ],
        out_shape=[
            jax.ShapeDtypeStruct(data.shape, jnp.bfloat16),
            jax.ShapeDtypeStruct((4 * channels, channels), jnp.bfloat16),
        ],
        scratch_shapes=[pltpu.VMEM((4, channels, channels), jnp.float32)]
        + [pltpu.VMEM((halves, tokens, LANES), jnp.float32)] * 3
        + [
            pltpu.VMEM((tokens, channels), jnp.bfloat16),
            pltpu.VMEM((tokens, 3 * channels), jnp.bfloat16),
        ],
        compiler_params=PARAMS,
        cost_estimate=pl.CostEstimate(
            flops=count * 2 * channels * 24 * channels,
            bytes_accessed=2 * count * channels * 10,
            transcendentals=0,
        ),
    )(data, cot, qkv, probs, context, *weights)


def run_kernel(data, gain1, wqkv, wout, pos_bias, gain2, wup, wdown):
    gain1, gain2, bias, mask, width = prepared(gain1, gain2, pos_bias, data.shape[-1])
    tokens, cot = data[:, :, :, 0], data[:, :, :, 1]
    mixed, qkv, probs, context = forward(
        tokens, gain1, wqkv, wout, bias, gain2, wup, wdown, mask, width
    )
    grad, p = backward(tokens, cot, qkv, probs, context, gain1, wqkv, wout, mask, width)
    p = p.astype(jnp.float32).reshape(4, 256, 256)
    return jnp.stack([mixed, grad], axis=3), jnp.concatenate([p[0], p[1], p[2]], axis=1), p[3]


def prepared(gain1, gain2, pos_bias, channels):
    heads, members, _ = pos_bias.shape
    width = channels // heads
    per = LANES // width
    halves = channels // LANES
    bias = (pos_bias * LOG2E).transpose(2, 0, 1).reshape(members, halves, per * members)
    bias = bias.transpose(1, 0, 2)
    row_head = lax.broadcasted_iota(jnp.int32, (per * members, LANES), 0) // members
    lane_head = lax.broadcasted_iota(jnp.int32, (per * members, LANES), 1) // width
    mask = (row_head == lane_head).astype(jnp.bfloat16)
    return gain1.reshape(1, -1), gain2.reshape(1, -1), bias, mask, width


def place_kernel(source_ref, out_ref):
    out_ref[...] = source_ref[...]


def placed(values):
    rows, columns, channels = values.shape
    block = pl.BlockSpec((rows // 4, columns, channels), lambda i: (i, 0, 0))
    return pl.pallas_call(
        place_kernel,
        grid=(4,),
        in_specs=[block],
        out_specs=block,
        out_shape=jax.ShapeDtypeStruct(values.shape, values.dtype),
        cost_estimate=pl.CostEstimate(
            flops=0, bytes_accessed=4 * values.size, transcendentals=0
        ),
    )(values)


def exchange(pieces):
    return lax.all_to_all(pieces, AXES, 0, 0, tiled=True)


def local(tokens, cotangent, norm1_gain, w_qkv, w_out, pos_bias, norm2_gain, w_up, w_down):
    tile_rows, tile_cols, channels = tokens.shape
    devices = lax.axis_size(AXES)
    classes = lax.axis_size("gy") // GRID
    positions = tile_rows * tile_cols // devices
    factor = 1.0 / math.sqrt(tile_rows * tile_cols * devices)
    gain1, gain2, bias, mask, width = prepared(norm1_gain, norm2_gain, pos_bias, channels)
    sent = (devices, positions, channels)
    kept = (GRID, classes, GRID, positions, channels)

    data = exchange(tokens.reshape(sent)).reshape(kept)
    cot = exchange(cotangent.reshape(sent)).reshape(kept)
    mixed, qkv, probs, context = forward(
        data, gain1, w_qkv, w_out, bias, gain2, w_up, w_down, mask, width
    )
    mixed = exchange(mixed.reshape(sent)).reshape(tokens.shape)
    grad, partial = backward(
        data, cot, qkv, probs, context, gain1, w_qkv, w_out, mask, width
    )
    pieces = partial.reshape(devices, -1, channels)
    joined = jnp.concatenate([grad.reshape(sent), pieces], axis=1)
    joined, mixed = lax.optimization_barrier((joined, mixed))
    joined = exchange(joined)
    total = jnp.sum(joined[:, positions:].astype(jnp.float32), axis=0) * factor
    total = exchange(jnp.broadcast_to(total.astype(jnp.bfloat16)[None], pieces.shape))
    blocks = total.astype(jnp.float32).reshape(4, channels, channels)
    grad_qkv = jnp.concatenate([blocks[0], blocks[1], blocks[2]], axis=1)
    grad_tokens = joined[:, :positions].reshape(tokens.shape)
    return (placed(mixed), grad_tokens, grad_qkv, blocks[3])


def solution(mesh):
    placed = (P("gy", "gx", None), P("gy", "gx", None), P(), P(), P(), P(), P(), P(), P())
    return jax.shard_map(
        local,
        mesh=mesh,
        in_specs=placed,
        out_specs=(P("gy", "gx", None), P("gy", "gx", None), P(), P()),
        check_vma=False,
    )
```

```python
import functools
import math

import jax
import jax.numpy as jnp
from jax import lax
from jax.experimental import pallas as pl
from jax.experimental.pallas import tpu as pltpu
from jax.sharding import PartitionSpec as P

GRID = 8
MEMBERS = GRID * GRID
EPSILON = 1e-05
LOG2E = math.log2(math.e)
AXES = ("gy", "gx")
LANES = 128
BLOCK = 16
DENSE = 8
UNROLL = 8
VMEM_LIMIT = 62 * 1024 * 1024 + 512 * 1024


def dot(a, b, contract=((1,), (0,))):
    return lax.dot_general(a, b, (contract, ((), ())), preferred_element_type=jnp.float32)


def normalize(wide, gain):
    centre = jnp.mean(wide, axis=-1, keepdims=True)
    shifted = wide - centre
    variance = jnp.mean(shifted * shifted, axis=-1, keepdims=True)
    inverse = lax.rsqrt(variance + EPSILON)
    unit = shifted * inverse
    return unit * gain, unit, inverse


def gelu(x):
    inner = x * (0.7978845608028654 + 0.035677408136300125 * (x * x))
    half = 0.5 * x
    return half + half * jnp.tanh(inner)


def pick_heads(full, lane_head, per):
    out = full[(per - 1) * MEMBERS : per * MEMBERS]
    for h in range(per - 2, -1, -1):
        out = jnp.where(lane_head == h, full[h * MEMBERS : (h + 1) * MEMBERS], out)
    return out


def load_tokens(scratch_ref, data_ref):
    halves, tokens, _ = scratch_ref.shape
    for j in range(halves):
        lanes = slice(j * LANES, (j + 1) * LANES)
        scratch_ref[j] = data_ref[:, 0, :, :, lanes].reshape(tokens, LANES).astype(jnp.float32)


def store_tokens(data_ref, scratch_ref):
    halves = scratch_ref.shape[0]
    for j in range(halves):
        lanes = slice(j * LANES, (j + 1) * LANES)
        wide = scratch_ref[j].reshape(GRID, GRID, BLOCK, LANES)
        data_ref[:, 0, :, :, lanes] = wide.astype(jnp.bfloat16)


def head_mask(shape, width):
    row_head = lax.broadcasted_iota(jnp.int32, shape, 0) // MEMBERS
    lane_head = lax.broadcasted_iota(jnp.int32, shape, 1) // width
    return (row_head == lane_head).astype(jnp.float32).astype(jnp.bfloat16)


def group_rows(i):
    return [pl.ds(i * DENSE + g, MEMBERS, stride=BLOCK) for g in range(DENSE)]


def token_rows(i):
    count = DENSE * MEMBERS
    return pl.ds(i * count, count)


def gather_groups(ref, rows):
    halves = ref.shape[0]
    return jnp.concatenate(
        [jnp.concatenate([ref[j, r, :] for j in range(halves)], axis=1) for r in rows], axis=0
    )


def scatter_groups(ref, rows, values):
    for g, r in enumerate(rows):
        for j in range(ref.shape[0]):
            ref[j, r, :] = values[g * MEMBERS : (g + 1) * MEMBERS, j * LANES : (j + 1) * LANES]


def repeat(count, step):
    for i in range(count):
        step(i)


def forward_kernel(
    width,
    data_ref,
    gain1_ref,
    wqkv_ref,
    wout_ref,
    pos_ref,
    gain2_ref,
    wup_ref,
    wdown_ref,
    out_ref,
    qkv_ref,
    probs_ref,
    context_ref,
    xs_ref,
    mixed_ref,
    mask_ref,
    bias_ref,
):
    channels = wout_ref.shape[0]
    halves = channels // LANES
    per = LANES // width
    scale = 1.0 / math.sqrt(width)
    @pl.when((pl.program_id(0) == 0) & (pl.program_id(1) == 0))
    def _():
        mask_ref[...] = head_mask(mask_ref.shape, width)
        for j in range(halves):
            for h in range(per):
                lanes = slice(h * MEMBERS, (h + 1) * MEMBERS)
                bias_ref[j, :, lanes] = pos_ref[j * per + h].T * LOG2E

    load_tokens(xs_ref, data_ref)
    lane_head = lax.broadcasted_iota(jnp.int32, (MEMBERS, LANES), 1) // width

    def project(i):
        x = gather_groups(xs_ref, group_rows(i))
        normed = normalize(x, gain1_ref[...])[0].astype(jnp.bfloat16)
        qkv_ref[token_rows(i), :] = dot(normed, wqkv_ref[...]).astype(jnp.bfloat16)

    def attend(i):
        units = []
        for g in range(UNROLL):
            part = pl.ds((i * UNROLL + g) * MEMBERS, MEMBERS)
            for j in range(halves):
                slot = (i * UNROLL + g) * halves + j
                units.append((part, j * LANES, j, pl.ds(slot * MEMBERS, MEMBERS)))
        scores, probs = [], []
        for part, at, j, slot in units:
            q = qkv_ref[part, at : at + LANES]
            k = qkv_ref[part, channels + at : channels + at + LANES]
            q_heads = jnp.concatenate([q] * per, axis=0) * mask_ref[...]
            scores.append(dot(k, q_heads, ((1,), (1,))))
        for (part, at, j, slot), raw in zip(units, scores):
            raw = raw * (scale * LOG2E) + bias_ref[j]
            e = jnp.exp2(raw - jnp.max(raw, axis=0, keepdims=True))
            low = (e * (1.0 / jnp.sum(e, axis=0, keepdims=True))).astype(jnp.bfloat16)
            probs_ref[slot, :] = low
            probs.append(low)
        for (part, at, j, slot), low in zip(units, probs):
            v = qkv_ref[part, 2 * channels + at : 2 * channels + at + LANES]
            context = pick_heads(dot(low, v, ((0,), (0,))), lane_head, per)
            context_ref[part, at : at + LANES] = context.astype(jnp.bfloat16)

    def finish(i):
        rows = group_rows(i)
        x = gather_groups(xs_ref, rows)
        context = context_ref[token_rows(i), :]
        attended = (x + dot(context, wout_ref[...])).astype(jnp.bfloat16).astype(jnp.float32)
        normed2 = normalize(attended, gain2_ref[...])[0].astype(jnp.bfloat16)
        mixed = attended
        wide = wup_ref.shape[1] // 2
        for f in range(2):
            at = slice(f * wide, (f + 1) * wide)
            hidden = gelu(dot(normed2, wup_ref[:, at])).astype(jnp.bfloat16)
            mixed = mixed + dot(hidden, wdown_ref[at, :])
        scatter_groups(mixed_ref, rows, mixed)

    project(0)
    project(1)
    attend(0)
    attend(1)
    finish(0)
    finish(1)
    store_tokens(out_ref, mixed_ref)


def backward_kernel(
    width,
    data_ref,
    cot_ref,
    qkv_ref,
    probs_ref,
    context_ref,
    gain1_ref,
    wqkv_ref,
    wout_ref,
    out_ref,
    acc_ref,
    xs_ref,
    gs_ref,
    grad_ref,
    dctx_ref,
    dqkv_ref,
    mask_ref,
    stage_ref,
    pieces_ref,
    sent,
    sent_pieces,
):
    channels = wout_ref.shape[0]
    halves = channels // LANES
    per = LANES // width
    scale = 1.0 / math.sqrt(width)

    steps = pl.num_programs(1)
    turn = pl.program_id(0) * steps + pl.program_id(1)
    last = pl.num_programs(0) * steps - 1
    positions = steps * BLOCK

    @pl.when(turn == 0)
    def _():
        acc_ref[...] = jnp.zeros_like(acc_ref)
        mask_ref[...] = head_mask(mask_ref.shape, width)

    load_tokens(xs_ref, data_ref)
    load_tokens(gs_ref, cot_ref)
    lane_head = lax.broadcasted_iota(jnp.int32, (MEMBERS, LANES), 1) // width

    def project(i):
        here = token_rows(i)
        cot = gather_groups(gs_ref, group_rows(i)).astype(jnp.bfloat16)
        dctx_ref[here, :] = dot(cot, wout_ref[...], ((1,), (1,))).astype(jnp.bfloat16)
        d_weight = dot(context_ref[here, :], cot, ((0,), (0,)))
        for n in range(halves):
            acc_ref[3 * halves + n] += d_weight[:, n * LANES : (n + 1) * LANES]

    def attend(i):
        units = []
        for g in range(UNROLL):
            part = pl.ds((i * UNROLL + g) * MEMBERS, MEMBERS)
            for j in range(halves):
                slot = (i * UNROLL + g) * halves + j
                units.append((part, j * LANES, pl.ds(slot * MEMBERS, MEMBERS)))

        def put(n, part, at, value):
            to = n * channels + at
            dqkv_ref[part, to : to + LANES] = value.astype(jnp.bfloat16)

        d_probs, d_scaled = [], []
        for part, at, slot in units:
            v = qkv_ref[part, 2 * channels + at : 2 * channels + at + LANES]
            dc_heads = jnp.concatenate([dctx_ref[part, at : at + LANES]] * per, axis=0) * mask_ref[...]
            d_probs.append(dot(v, dc_heads, ((1,), (1,))))
            put(2, part, at, dot(probs_ref[slot, :], dc_heads))
        for (part, at, slot), dp in zip(units, d_probs):
            probs = probs_ref[slot, :].astype(jnp.float32)
            delta = jnp.sum(probs * dp, axis=0, keepdims=True)
            d_scaled.append((probs * (dp - delta) * scale).astype(jnp.bfloat16))
        for (part, at, slot), ds in zip(units, d_scaled):
            q_heads = jnp.concatenate([qkv_ref[part, at : at + LANES]] * per, axis=0) * mask_ref[...]
            put(1, part, at, dot(ds, q_heads))
            k = qkv_ref[part, channels + at : channels + at + LANES]
            put(0, part, at, pick_heads(dot(ds, k, ((0,), (0,))), lane_head, per))

    def finish(i):
        rows = group_rows(i)
        x = gather_groups(xs_ref, rows)
        d_qkv = dqkv_ref[token_rows(i), :]
        normed_wide, unit, inverse = normalize(x, gain1_ref[...])
        d_weight = dot(normed_wide.astype(jnp.bfloat16), d_qkv, ((0,), (0,)))
        for n in range(3 * halves):
            acc_ref[n] += d_weight[:, n * LANES : (n + 1) * LANES]
        d_unit = dot(d_qkv, wqkv_ref[...], ((1,), (1,))) * gain1_ref[...]
        grad = gather_groups(gs_ref, rows) + inverse * (
            d_unit
            - jnp.mean(d_unit, axis=-1, keepdims=True)
            - unit * jnp.mean(d_unit * unit, axis=-1, keepdims=True)
        )
        scatter_groups(grad_ref, rows, grad)

    project(0)
    project(1)
    attend(0)
    attend(1)
    finish(0)
    finish(1)

    def send(n, j):
        rows = pl.ds(j * positions + n % steps * BLOCK, BLOCK)
        return pltpu.make_async_copy(
            stage_ref.at[n % 2, j], out_ref.at[:, n // steps, :, rows, :], sent.at[n % 2, j]
        )

    @pl.when(turn >= 2)
    def _():
        for j in range(halves):
            send(turn - 2, j).wait()

    for j in range(halves):
        wide = grad_ref[j].reshape(GRID, GRID, BLOCK, LANES)
        stage_ref[turn % 2, j] = wide.astype(jnp.bfloat16)
        send(turn, j).start()

    @pl.when(turn == last)
    def _():
        pieces_ref[...] = acc_ref[...].reshape(pieces_ref.shape).astype(jnp.bfloat16)
        tail = pltpu.make_async_copy(
            pieces_ref,
            out_ref.at[:, :, :, pl.ds(halves * positions, pieces_ref.shape[3]), :],
            sent_pieces,
        )
        tail.start()
        for j in range(halves):
            send(turn - 1, j).wait()
        for j in range(halves):
            send(turn, j).wait()
        tail.wait()


def specs(data):
    _, classes, _, positions, channels = data.shape
    steps = positions // BLOCK
    grid = (classes, steps)
    block = pl.BlockSpec((GRID, 1, GRID, BLOCK, channels), lambda c, p: (0, c, 0, p, 0))
    whole = lambda a: pl.BlockSpec(a.shape, lambda c, p: (0,) * a.ndim)
    flat = lambda rows, width: pl.BlockSpec((rows, width), lambda c, p: (c * steps + p, 0))
    return grid, block, whole, flat, classes * positions


PARAMS = pltpu.CompilerParams(vmem_limit_bytes=VMEM_LIMIT)


def forward(data, gain1, wqkv, wout, pos_bias, gain2, wup, wdown, width):
    grid, block, whole, flat, groups = specs(data)
    channels = data.shape[-1]
    halves = channels // LANES
    tokens = MEMBERS * BLOCK
    count = groups * MEMBERS
    ff = wup.shape[1]
    row_width = LANES // width * MEMBERS
    weights = (gain1, wqkv, wout, pos_bias, gain2, wup, wdown)
    return pl.pallas_call(
        functools.partial(forward_kernel, width),
        grid=grid,
        in_specs=[block] + [whole(a) for a in weights],
        out_specs=[
            block,
            flat(tokens, 3 * channels),
            flat(tokens * halves, row_width),
            flat(tokens, channels),
        ],
        out_shape=[
            jax.ShapeDtypeStruct(data.shape, jnp.bfloat16),
            jax.ShapeDtypeStruct((count, 3 * channels), jnp.bfloat16),
            jax.ShapeDtypeStruct((count * halves, row_width), jnp.bfloat16),
            jax.ShapeDtypeStruct((count, channels), jnp.bfloat16),
        ],
        scratch_shapes=[pltpu.VMEM((halves, tokens, LANES), jnp.float32)] * 2
        + [
            pltpu.VMEM((row_width, LANES), jnp.bfloat16),
            pltpu.VMEM((halves, MEMBERS, row_width), jnp.float32),
        ],
        compiler_params=PARAMS,
        cost_estimate=pl.CostEstimate(
            flops=count * 2 * channels * (16 * channels + 2 * ff),
            bytes_accessed=2 * count * channels * 8,
            transcendentals=count * ff,
        ),
    )(data, *weights)


def backward(data, cot, qkv, probs, context, gain1, wqkv, wout, width):
    grid, block, whole, flat, groups = specs(data)
    channels = data.shape[-1]
    halves = channels // LANES
    tokens = MEMBERS * BLOCK
    count = groups * MEMBERS
    row_width = LANES // width * MEMBERS
    devices = GRID * GRID * data.shape[1]
    positions = data.shape[3]
    piece = 4 * halves * channels // devices
    rows = halves * positions + piece
    weights = (gain1, wqkv, wout)
    return pl.pallas_call(
        functools.partial(backward_kernel, width),
        grid=grid,
        in_specs=[
            block,
            block,
            flat(tokens, 3 * channels),
            flat(tokens * halves, row_width),
            flat(tokens, channels),
        ]
        + [whole(a) for a in weights],
        out_specs=pl.BlockSpec(memory_space=pl.ANY),
        out_shape=jax.ShapeDtypeStruct(data.shape[:3] + (rows, LANES), jnp.bfloat16),
        scratch_shapes=[pltpu.VMEM((4 * halves, channels, LANES), jnp.float32)]
        + [pltpu.VMEM((halves, tokens, LANES), jnp.float32)] * 3
        + [
            pltpu.VMEM((tokens, channels), jnp.bfloat16),
            pltpu.VMEM((tokens, 3 * channels), jnp.bfloat16),
            pltpu.VMEM((row_width, LANES), jnp.bfloat16),
            pltpu.VMEM((2, halves, GRID, GRID, BLOCK, LANES), jnp.bfloat16),
            pltpu.VMEM(data.shape[:3] + (piece, LANES), jnp.bfloat16),
            pltpu.SemaphoreType.DMA((2, halves)),
            pltpu.SemaphoreType.DMA,
        ],
        compiler_params=PARAMS,
        cost_estimate=pl.CostEstimate(
            flops=count * 2 * channels * 24 * channels,
            bytes_accessed=2 * count * channels * 10,
            transcendentals=0,
        ),
    )(data, cot, qkv, probs, context, *weights)


def place_kernel(source_ref, out_ref):
    out_ref[...] = source_ref[...]


def placed(values):
    rows, columns, channels = values.shape
    block = pl.BlockSpec((rows // 4, columns, channels), lambda i: (i, 0, 0))
    return pl.pallas_call(
        place_kernel,
        grid=(4,),
        in_specs=[block],
        out_specs=block,
        out_shape=jax.ShapeDtypeStruct(values.shape, values.dtype),
        cost_estimate=pl.CostEstimate(
            flops=0, bytes_accessed=4 * values.size, transcendentals=0
        ),
    )(values)


def join_kernel(halves, source_ref, out_ref):
    rows, columns, channels = out_ref.shape
    devices = source_ref.shape[0]
    positions = rows * columns // devices
    for j in range(halves):
        part = source_ref[:, j * positions : (j + 1) * positions, :]
        out_ref[:, :, j * LANES : (j + 1) * LANES] = part.reshape(rows, columns, LANES)


def joined_halves(values, shape):
    rows, columns, channels = shape
    devices, height, _ = values.shape
    return pl.pallas_call(
        functools.partial(join_kernel, channels // LANES),
        grid=(4,),
        in_specs=[pl.BlockSpec((devices // 4, height, LANES), lambda i: (i, 0, 0))],
        out_specs=pl.BlockSpec((rows // 4, columns, channels), lambda i: (i, 0, 0)),
        out_shape=jax.ShapeDtypeStruct(shape, values.dtype),
        cost_estimate=pl.CostEstimate(
            flops=0, bytes_accessed=4 * values.size, transcendentals=0
        ),
    )(values)


def by_blocks(pieces, channels):
    blocks = pieces.astype(jnp.float32).reshape(-1, channels, LANES)
    split = 3 * channels // LANES
    return (
        jnp.concatenate([blocks[n] for n in range(split)], axis=1),
        jnp.concatenate([blocks[n] for n in range(split, blocks.shape[0])], axis=1),
    )


def exchange(pieces):
    return lax.all_to_all(pieces, AXES, 0, 0, tiled=True)


def local(tokens, cotangent, norm1_gain, w_qkv, w_out, pos_bias, norm2_gain, w_up, w_down):
    tile_rows, tile_cols, channels = tokens.shape
    devices = lax.axis_size(AXES)
    classes = lax.axis_size("gy") // GRID
    positions = tile_rows * tile_cols // devices
    factor = 1.0 / math.sqrt(tile_rows * tile_cols * devices)
    width = channels // pos_bias.shape[0]
    own = positions * channels // LANES
    gain1, gain2 = norm1_gain.reshape(1, -1), norm2_gain.reshape(1, -1)
    sent = (devices, positions, channels)
    kept = (GRID, classes, GRID, positions, channels)

    data = exchange(tokens.reshape(sent)).reshape(kept)
    cot = exchange(cotangent.reshape(sent)).reshape(kept)
    mixed, qkv, probs, context = forward(
        data, gain1, w_qkv, w_out, pos_bias, gain2, w_up, w_down, width
    )
    mixed = exchange(mixed.reshape(sent)).reshape(tokens.shape)
    grad = backward(data, cot, qkv, probs, context, gain1, w_qkv, w_out, width)
    grad, mixed = lax.optimization_barrier((grad.reshape(devices, -1, LANES), mixed))
    grad = exchange(grad)
    total = jnp.sum(grad[:, own:].astype(jnp.float32), axis=0) * factor
    total = jnp.broadcast_to(total.astype(jnp.bfloat16)[None], (devices,) + total.shape)
    grad_qkv, grad_out = by_blocks(exchange(total), channels)
    return (placed(mixed), joined_halves(grad, tokens.shape), grad_qkv, grad_out)


def solution(mesh):
    placed = (P("gy", "gx", None), P("gy", "gx", None), P(), P(), P(), P(), P(), P(), P())
    return jax.shard_map(
        local,
        mesh=mesh,
        in_specs=placed,
        out_specs=(P("gy", "gx", None), P("gy", "gx", None), P(), P()),
        check_vma=False,
    )
```

```python
import functools
import math

import jax
import jax.numpy as jnp
from jax import lax
from jax.experimental import pallas as pl
from jax.experimental.pallas import tpu as pltpu
from jax.sharding import PartitionSpec as P

GRID = 8
CORES = 2
MEMBERS = GRID * GRID
EPSILON = 1e-05
LOG2E = math.log2(math.e)
AXES = ("gy", "gx")
LANES = 128
BLOCK = 16
DENSE = 8
UNROLL = 8
VMEM_LIMIT = 36 * 1024 * 1024


def dot(a, b, contract=((1,), (0,))):
    return lax.dot_general(a, b, (contract, ((), ())), preferred_element_type=jnp.float32)


def normalize(wide, gain):
    centre = jnp.mean(wide, axis=-1, keepdims=True)
    shifted = wide - centre
    variance = jnp.mean(shifted * shifted, axis=-1, keepdims=True)
    inverse = lax.rsqrt(variance + EPSILON)
    unit = shifted * inverse
    return unit * gain, unit, inverse


def gelu(x):
    inner = x * (0.7978845608028654 + 0.035677408136300125 * (x * x))
    half = 0.5 * x
    return half + half * jnp.tanh(inner)


def pick_heads(full, lane_head, per):
    out = full[(per - 1) * MEMBERS : per * MEMBERS]
    for h in range(per - 2, -1, -1):
        out = jnp.where(lane_head == h, full[h * MEMBERS : (h + 1) * MEMBERS], out)
    return out


def load_tokens(scratch_ref, data_ref):
    halves, tokens, _ = scratch_ref.shape
    for j in range(halves):
        lanes = slice(j * LANES, (j + 1) * LANES)
        scratch_ref[j] = data_ref[:, 0, :, :, lanes].reshape(tokens, LANES).astype(jnp.float32)


def store_tokens(data_ref, scratch_ref):
    halves = scratch_ref.shape[0]
    for j in range(halves):
        lanes = slice(j * LANES, (j + 1) * LANES)
        wide = scratch_ref[j].reshape(GRID, GRID, BLOCK, LANES)
        data_ref[:, 0, :, :, lanes] = wide.astype(jnp.bfloat16)


def head_mask(shape, width):
    row_head = lax.broadcasted_iota(jnp.int32, shape, 0) // MEMBERS
    lane_head = lax.broadcasted_iota(jnp.int32, shape, 1) // width
    return (row_head == lane_head).astype(jnp.float32).astype(jnp.bfloat16)


def group_rows(i):
    return [pl.ds(i * DENSE + g, MEMBERS, stride=BLOCK) for g in range(DENSE)]


def token_rows(i):
    count = DENSE * MEMBERS
    return pl.ds(i * count, count)


def gather_groups(ref, rows):
    halves = ref.shape[0]
    return jnp.concatenate(
        [jnp.concatenate([ref[j, r, :] for j in range(halves)], axis=1) for r in rows], axis=0
    )


def scatter_groups(ref, rows, values):
    for g, r in enumerate(rows):
        for j in range(ref.shape[0]):
            ref[j, r, :] = values[g * MEMBERS : (g + 1) * MEMBERS, j * LANES : (j + 1) * LANES]


def repeat(count, step):
    for i in range(count):
        step(i)


def forward_kernel(
    width,
    data_ref,
    gain1_ref,
    wqkv_ref,
    wout_ref,
    pos_ref,
    gain2_ref,
    wup_ref,
    wdown_ref,
    out_ref,
    qkv_ref,
    probs_ref,
    context_ref,
    xs_ref,
    mixed_ref,
    mask_ref,
    bias_ref,
):
    channels = wout_ref.shape[0]
    halves = channels // LANES
    per = LANES // width
    scale = 1.0 / math.sqrt(width)
    @pl.when((pl.program_id(0) == 0) & (pl.program_id(1) == 0))
    def _():
        mask_ref[...] = head_mask(mask_ref.shape, width)
        for j in range(halves):
            for h in range(per):
                lanes = slice(h * MEMBERS, (h + 1) * MEMBERS)
                bias_ref[j, :, lanes] = pos_ref[j * per + h].T * LOG2E

    load_tokens(xs_ref, data_ref)
    lane_head = lax.broadcasted_iota(jnp.int32, (MEMBERS, LANES), 1) // width

    def project(i):
        x = gather_groups(xs_ref, group_rows(i))
        normed = normalize(x, gain1_ref[...])[0].astype(jnp.bfloat16)
        qkv_ref[token_rows(i), :] = dot(normed, wqkv_ref[...]).astype(jnp.bfloat16)

    def attend(i):
        units = []
        for g in range(UNROLL):
            part = pl.ds((i * UNROLL + g) * MEMBERS, MEMBERS)
            for j in range(halves):
                slot = (i * UNROLL + g) * halves + j
                units.append((part, j * LANES, j, pl.ds(slot * MEMBERS, MEMBERS)))
        scores, probs = [], []
        for part, at, j, slot in units:
            q = qkv_ref[part, at : at + LANES]
            k = qkv_ref[part, channels + at : channels + at + LANES]
            q_heads = jnp.concatenate([q] * per, axis=0) * mask_ref[...]
            scores.append(dot(k, q_heads, ((1,), (1,))))
        for (part, at, j, slot), raw in zip(units, scores):
            raw = raw * (scale * LOG2E) + bias_ref[j]
            e = jnp.exp2(raw - jnp.max(raw, axis=0, keepdims=True))
            low = (e * (1.0 / jnp.sum(e, axis=0, keepdims=True))).astype(jnp.bfloat16)
            probs_ref[slot, :] = low
            probs.append(low)
        for (part, at, j, slot), low in zip(units, probs):
            v = qkv_ref[part, 2 * channels + at : 2 * channels + at + LANES]
            context = pick_heads(dot(low, v, ((0,), (0,))), lane_head, per)
            context_ref[part, at : at + LANES] = context.astype(jnp.bfloat16)

    def finish(i):
        rows = group_rows(i)
        x = gather_groups(xs_ref, rows)
        context = context_ref[token_rows(i), :]
        attended = (x + dot(context, wout_ref[...])).astype(jnp.bfloat16).astype(jnp.float32)
        normed2 = normalize(attended, gain2_ref[...])[0].astype(jnp.bfloat16)
        mixed = attended
        wide = wup_ref.shape[1] // 2
        for f in range(2):
            at = slice(f * wide, (f + 1) * wide)
            hidden = gelu(dot(normed2, wup_ref[:, at])).astype(jnp.bfloat16)
            mixed = mixed + dot(hidden, wdown_ref[at, :])
        scatter_groups(mixed_ref, rows, mixed)

    project(0)
    project(1)
    attend(0)
    attend(1)
    finish(0)
    finish(1)
    store_tokens(out_ref, mixed_ref)


def backward_kernel(
    width,
    core_ref,
    data_ref,
    cot_ref,
    qkv_ref,
    probs_ref,
    context_ref,
    gain1_ref,
    wqkv_ref,
    wout_ref,
    out_ref,
    own_ref,
    other_ref,
    acc_ref,
    xs_ref,
    gs_ref,
    grad_ref,
    dctx_ref,
    dqkv_ref,
    mask_ref,
    stage_ref,
    sent,
):
    channels = wout_ref.shape[0]
    halves = channels // LANES
    per = LANES // width
    scale = 1.0 / math.sqrt(width)

    steps = pl.num_programs(1)
    turn = pl.program_id(0) * steps + pl.program_id(1)
    last = pl.num_programs(0) * steps - 1

    @pl.when(turn == 0)
    def _():
        acc_ref[...] = jnp.zeros_like(acc_ref)
        mask_ref[...] = head_mask(mask_ref.shape, width)

    load_tokens(xs_ref, data_ref)
    load_tokens(gs_ref, cot_ref)
    lane_head = lax.broadcasted_iota(jnp.int32, (MEMBERS, LANES), 1) // width

    def project(i):
        here = token_rows(i)
        cot = gather_groups(gs_ref, group_rows(i)).astype(jnp.bfloat16)
        dctx_ref[here, :] = dot(cot, wout_ref[...], ((1,), (1,))).astype(jnp.bfloat16)
        acc_ref[3] += dot(context_ref[here, :], cot, ((0,), (0,)))

    def attend(i):
        units = []
        for g in range(UNROLL):
            part = pl.ds((i * UNROLL + g) * MEMBERS, MEMBERS)
            for j in range(halves):
                slot = (i * UNROLL + g) * halves + j
                units.append((part, j * LANES, pl.ds(slot * MEMBERS, MEMBERS)))

        def put(n, part, at, value):
            to = n * channels + at
            dqkv_ref[part, to : to + LANES] = value.astype(jnp.bfloat16)

        d_probs, d_scaled = [], []
        for part, at, slot in units:
            v = qkv_ref[part, 2 * channels + at : 2 * channels + at + LANES]
            dc_heads = jnp.concatenate([dctx_ref[part, at : at + LANES]] * per, axis=0) * mask_ref[...]
            d_probs.append(dot(v, dc_heads, ((1,), (1,))))
            put(2, part, at, dot(probs_ref[slot, :], dc_heads))
        for (part, at, slot), dp in zip(units, d_probs):
            probs = probs_ref[slot, :].astype(jnp.float32)
            delta = jnp.sum(probs * dp, axis=0, keepdims=True)
            delta = delta / jnp.sum(probs, axis=0, keepdims=True)
            d_scaled.append((probs * (dp - delta) * scale).astype(jnp.bfloat16))
        for (part, at, slot), ds in zip(units, d_scaled):
            q_heads = jnp.concatenate([qkv_ref[part, at : at + LANES]] * per, axis=0) * mask_ref[...]
            put(1, part, at, dot(ds, q_heads))
            k = qkv_ref[part, channels + at : channels + at + LANES]
            put(0, part, at, pick_heads(dot(ds, k, ((0,), (0,))), lane_head, per))

    def finish(i):
        rows = group_rows(i)
        x = gather_groups(xs_ref, rows)
        d_qkv = dqkv_ref[token_rows(i), :]
        normed_wide, unit, inverse = normalize(x, gain1_ref[...])
        d_weight = dot(normed_wide.astype(jnp.bfloat16), d_qkv, ((0,), (0,)))
        for n in range(3):
            acc_ref[n] += d_weight[:, n * channels : (n + 1) * channels]
        d_unit = dot(d_qkv, wqkv_ref[...], ((1,), (1,))) * gain1_ref[...]
        grad = gather_groups(gs_ref, rows) + inverse * (
            d_unit
            - jnp.mean(d_unit, axis=-1, keepdims=True)
            - unit * jnp.mean(d_unit * unit, axis=-1, keepdims=True)
        )
        scatter_groups(grad_ref, rows, grad)

    project(0)
    project(1)
    attend(0)
    attend(1)
    finish(0)
    finish(1)

    def send(n):
        rows = pl.ds(n % steps * BLOCK, BLOCK)
        return pltpu.make_async_copy(
            stage_ref.at[n % 2], out_ref.at[:, n // steps, :, rows, :], sent.at[n % 2]
        )

    @pl.when(turn >= 2)
    def _():
        send(turn - 2).wait()

    for j in range(halves):
        wide = grad_ref[j].reshape(GRID, GRID, BLOCK, LANES)
        stage_ref[turn % 2, :, :, :, j * LANES : (j + 1) * LANES] = wide.astype(jnp.bfloat16)
    send(turn).start()

    @pl.when(turn == last)
    def _():
        count = own_ref.shape[0] // GRID
        halved = acc_ref[...].reshape(GRID, CORES, count, channels).astype(jnp.bfloat16)
        first, second = (halved[:, c].reshape(own_ref.shape) for c in range(CORES))

        @pl.when(core_ref[0] == 0)
        def _():
            own_ref[...] = first
            other_ref[...] = second

        @pl.when(core_ref[0] == 1)
        def _():
            own_ref[...] = second
            other_ref[...] = first

        send(turn - 1).wait()
        send(turn).wait()


def specs(data):
    _, classes, _, positions, channels = data.shape
    steps = positions // BLOCK
    grid = (classes, steps)
    block = pl.BlockSpec((GRID, 1, GRID, BLOCK, channels), lambda c, p: (0, c, 0, p, 0))
    whole = lambda a: pl.BlockSpec(a.shape, lambda c, p: (0,) * a.ndim)
    flat = lambda rows, width: pl.BlockSpec((rows, width), lambda c, p: (c * steps + p, 0))
    return grid, block, whole, flat, classes * positions


PARAMS = pltpu.CompilerParams(vmem_limit_bytes=VMEM_LIMIT)


def forward(data, gain1, wqkv, wout, pos_bias, gain2, wup, wdown, width):
    grid, block, whole, flat, groups = specs(data)
    channels = data.shape[-1]
    halves = channels // LANES
    tokens = MEMBERS * BLOCK
    count = groups * MEMBERS
    ff = wup.shape[1]
    row_width = LANES // width * MEMBERS
    weights = (gain1, wqkv, wout, pos_bias, gain2, wup, wdown)
    return pl.pallas_call(
        functools.partial(forward_kernel, width),
        grid=grid,
        in_specs=[block] + [whole(a) for a in weights],
        out_specs=[
            block,
            flat(tokens, 3 * channels),
            flat(tokens * halves, row_width),
            flat(tokens, channels),
        ],
        out_shape=[
            pltpu.VMEM(data.shape, jnp.bfloat16),
            pltpu.HBM((count, 3 * channels), jnp.bfloat16),
            pltpu.HBM((count * halves, row_width), jnp.bfloat16),
            pltpu.HBM((count, channels), jnp.bfloat16),
        ],
        scratch_shapes=[pltpu.VMEM((halves, tokens, LANES), jnp.float32)] * 2
        + [
            pltpu.VMEM((row_width, LANES), jnp.bfloat16),
            pltpu.VMEM((halves, MEMBERS, row_width), jnp.float32),
        ],
        compiler_params=PARAMS,
        cost_estimate=pl.CostEstimate(
            flops=count * 2 * channels * (16 * channels + 2 * ff),
            bytes_accessed=2 * count * channels * 8,
            transcendentals=count * ff,
        ),
    )(data, *weights)


def backward(core, data, cot, qkv, probs, context, gain1, wqkv, wout, width):
    grid, block, whole, flat, groups = specs(data)
    channels = data.shape[-1]
    halves = channels // LANES
    tokens = MEMBERS * BLOCK
    count = groups * MEMBERS
    row_width = LANES // width * MEMBERS
    rows = data.shape[3] + 4 * channels // (GRID * CORES * GRID)
    pieces = (4 * channels // CORES, channels)
    qkv, probs, context = (
        pltpu.with_memory_space_constraint(a, pltpu.HBM) for a in (qkv, probs, context)
    )
    cot = pltpu.with_memory_space_constraint(cot, pltpu.HBM)
    weights = (gain1, wqkv, wout)
    return pl.pallas_call(
        functools.partial(backward_kernel, width),
        grid=grid,
        in_specs=[
            pl.BlockSpec(memory_space=pltpu.SMEM),
            block,
            block,
            flat(tokens, 3 * channels),
            flat(tokens * halves, row_width),
            flat(tokens, channels),
        ]
        + [whole(a) for a in weights],
        out_specs=[
            pl.BlockSpec(memory_space=pl.ANY),
            pl.BlockSpec(pieces, lambda c, p: (0, 0)),
            pl.BlockSpec(pieces, lambda c, p: (0, 0)),
        ],
        out_shape=[
            pltpu.VMEM(data.shape[:3] + (rows, channels), jnp.bfloat16),
            jax.ShapeDtypeStruct(pieces, jnp.bfloat16),
            jax.ShapeDtypeStruct(pieces, jnp.bfloat16),
        ],
        scratch_shapes=[pltpu.VMEM((4, channels, channels), jnp.float32)]
        + [pltpu.VMEM((halves, tokens, LANES), jnp.float32)] * 3
        + [
            pltpu.VMEM((tokens, channels), jnp.bfloat16),
            pltpu.VMEM((tokens, 3 * channels), jnp.bfloat16),
            pltpu.VMEM((row_width, LANES), jnp.bfloat16),
            pltpu.VMEM((2, GRID, GRID, BLOCK, channels), jnp.bfloat16),
            pltpu.SemaphoreType.DMA((2,)),
        ],
        compiler_params=PARAMS,
        cost_estimate=pl.CostEstimate(
            flops=count * 2 * channels * 24 * channels,
            bytes_accessed=2 * count * channels * 10,
            transcendentals=0,
        ),
    )(core, data, cot, qkv, probs, context, *weights)


def place_kernel(source_ref, out_ref):
    out_ref[...] = source_ref[...]


def placed(values, space=None):
    rows, columns, channels = values.shape
    block = pl.BlockSpec((rows // 4, columns, channels), lambda i: (i, 0, 0))
    return pl.pallas_call(
        place_kernel,
        grid=(4,),
        in_specs=[block],
        out_specs=block,
        out_shape=(space or jax.ShapeDtypeStruct)(values.shape, values.dtype),
        cost_estimate=pl.CostEstimate(
            flops=0, bytes_accessed=4 * values.size, transcendentals=0
        ),
    )(values)


def trim_kernel(source_ref, out_ref):
    rows, columns, channels = out_ref.shape
    positions = rows * columns // source_ref.shape[0]
    out_ref[...] = source_ref[:, :positions, :].reshape(out_ref.shape)


def trimmed(values, shape):
    rows, columns, channels = shape
    devices, height, _ = values.shape
    values = pltpu.with_memory_space_constraint(values, pltpu.VMEM)
    return pl.pallas_call(
        trim_kernel,
        grid=(4,),
        in_specs=[pl.BlockSpec((devices // 4, height, channels), lambda i: (i, 0, 0))],
        out_specs=pl.BlockSpec((rows // 4, columns, channels), lambda i: (i, 0, 0)),
        out_shape=jax.ShapeDtypeStruct(shape, values.dtype),
        cost_estimate=pl.CostEstimate(
            flops=0, bytes_accessed=4 * values.size, transcendentals=0
        ),
    )(values)


def local(tokens, cotangent, norm1_gain, w_qkv, w_out, pos_bias, norm2_gain, w_up, w_down):
    tile_rows, tile_cols, channels = tokens.shape
    columns = lax.axis_size("gx")
    devices = lax.axis_size(AXES)
    core = lax.axis_index("gy") % CORES
    positions = tile_rows * tile_cols // MEMBERS
    factor = 1.0 / math.sqrt(tile_rows * tile_cols * devices)
    width = channels // pos_bias.shape[0]
    gain1, gain2 = norm1_gain.reshape(1, -1), norm2_gain.reshape(1, -1)
    sent = (MEMBERS, positions, channels)
    kept = (GRID, 1, GRID, positions, channels)
    def device(row, c, column):
        return (row * CORES + c) * columns + column

    members = [(row, column) for row in range(GRID) for column in range(GRID)]
    peers = [[device(row, c, column) for row, column in members] for c in range(CORES)]
    partner = [
        (device(row, c, column), device(row, 1 - c, column))
        for row, column in members
        for c in range(CORES)
    ]

    def exchange(pieces):
        return lax.all_to_all(pieces, AXES, 0, 0, axis_index_groups=peers, tiled=True)

    data = exchange(tokens.reshape(sent)).reshape(kept)
    cot = exchange(placed(cotangent, pltpu.VMEM).reshape(sent)).reshape(kept)
    mixed, qkv, probs, context = forward(
        data, gain1, w_qkv, w_out, pos_bias, gain2, w_up, w_down, width
    )
    mixed = exchange(mixed.reshape(sent)).reshape(tokens.shape)
    grad, own_pieces, other_pieces = backward(
        core.reshape(1), data, cot, qkv, probs, context, gain1, w_qkv, w_out, width
    )
    pair = own_pieces.astype(jnp.float32) + lax.ppermute(
        other_pieces, AXES, partner
    ).astype(jnp.float32)
    pair = pair.astype(jnp.bfloat16).reshape(GRID, 1, GRID, -1, channels)
    grad = lax.dynamic_update_slice(grad, pair, (0, 0, 0, positions, 0))
    grad, mixed = lax.optimization_barrier((grad.reshape(MEMBERS, -1, channels), mixed))
    grad = exchange(grad)
    total = jnp.sum(grad[:, positions:].astype(jnp.float32), axis=0) * factor
    total = jnp.broadcast_to(total.astype(jnp.bfloat16)[None], (devices,) + total.shape)
    total, grad = lax.optimization_barrier((total, grad))
    total = lax.all_to_all(total, AXES, 0, 0, tiled=True)
    blocks = total.astype(jnp.float32).reshape(4, channels, channels)
    grad_qkv = jnp.concatenate([blocks[0], blocks[1], blocks[2]], axis=1)
    return (placed(mixed), trimmed(grad, tokens.shape), grad_qkv, blocks[3])


def solution(mesh):
    placed = (P("gy", "gx", None), P("gy", "gx", None), P(), P(), P(), P(), P(), P(), P())
    return jax.shard_map(
        local,
        mesh=mesh,
        in_specs=placed,
        out_specs=(P("gy", "gx", None), P("gy", "gx", None), P(), P()),
        check_vma=False,
    )
```

```python
import functools
import math

import jax
import jax.numpy as jnp
from jax import lax
from jax.experimental import pallas as pl
from jax.experimental.pallas import tpu as pltpu
from jax.sharding import PartitionSpec as P

GRID = 8
CORES = 2
MEMBERS = GRID * GRID
EPSILON = 1e-05
LOG2E = math.log2(math.e)
AXES = ("gy", "gx")
LANES = 128
BLOCK = 16
DENSE = 8
UNROLL = 8
VMEM_LIMIT = 36 * 1024 * 1024


def dot(a, b, contract=((1,), (0,))):
    return lax.dot_general(a, b, (contract, ((), ())), preferred_element_type=jnp.float32)


def normalize(wide, gain):
    centre = jnp.mean(wide, axis=-1, keepdims=True)
    shifted = wide - centre
    variance = jnp.mean(shifted * shifted, axis=-1, keepdims=True)
    inverse = lax.rsqrt(variance + EPSILON)
    unit = shifted * inverse
    return unit * gain, unit, inverse


def gelu(x):
    inner = x * (0.7978845608028654 + 0.035677408136300125 * (x * x))
    half = 0.5 * x
    return half + half * jnp.tanh(inner)


def pick_heads(full, lane_head, per):
    out = full[(per - 1) * MEMBERS : per * MEMBERS]
    for h in range(per - 2, -1, -1):
        out = jnp.where(lane_head == h, full[h * MEMBERS : (h + 1) * MEMBERS], out)
    return out


def load_tokens(scratch_ref, data_ref):
    halves, tokens, _ = scratch_ref.shape
    for j in range(halves):
        lanes = slice(j * LANES, (j + 1) * LANES)
        scratch_ref[j] = data_ref[:, 0, :, :, lanes].reshape(tokens, LANES).astype(jnp.float32)


def store_tokens(data_ref, scratch_ref):
    halves = scratch_ref.shape[0]
    for j in range(halves):
        lanes = slice(j * LANES, (j + 1) * LANES)
        wide = scratch_ref[j].reshape(GRID, GRID, BLOCK, LANES)
        data_ref[:, 0, :, :, lanes] = wide.astype(jnp.bfloat16)


def head_mask(shape, width):
    row_head = lax.broadcasted_iota(jnp.int32, shape, 0) // MEMBERS
    lane_head = lax.broadcasted_iota(jnp.int32, shape, 1) // width
    return (row_head == lane_head).astype(jnp.float32).astype(jnp.bfloat16)


def group_rows(i):
    return [pl.ds(i * DENSE + g, MEMBERS, stride=BLOCK) for g in range(DENSE)]


def token_rows(i):
    count = DENSE * MEMBERS
    return pl.ds(i * count, count)


def gather_groups(ref, rows):
    halves = ref.shape[0]
    return jnp.concatenate(
        [jnp.concatenate([ref[j, r, :] for j in range(halves)], axis=1) for r in rows], axis=0
    )


def scatter_groups(ref, rows, values):
    for g, r in enumerate(rows):
        for j in range(ref.shape[0]):
            ref[j, r, :] = values[g * MEMBERS : (g + 1) * MEMBERS, j * LANES : (j + 1) * LANES]


def repeat(count, step):
    for i in range(count):
        step(i)


def forward_kernel(
    width,
    data_ref,
    gain1_ref,
    wqkv_ref,
    wout_ref,
    pos_ref,
    gain2_ref,
    wup_ref,
    wdown_ref,
    out_ref,
    qkv_ref,
    probs_ref,
    context_ref,
    xs_ref,
    mixed_ref,
    mask_ref,
    bias_ref,
):
    channels = wout_ref.shape[0]
    halves = channels // LANES
    per = LANES // width
    scale = 1.0 / math.sqrt(width)
    @pl.when((pl.program_id(0) == 0) & (pl.program_id(1) == 0))
    def _():
        mask_ref[...] = head_mask(mask_ref.shape, width)
        for j in range(halves):
            for h in range(per):
                lanes = slice(h * MEMBERS, (h + 1) * MEMBERS)
                bias_ref[j, :, lanes] = pos_ref[j * per + h].T * LOG2E

    load_tokens(xs_ref, data_ref)
    lane_head = lax.broadcasted_iota(jnp.int32, (MEMBERS, LANES), 1) // width

    def project(i):
        x = gather_groups(xs_ref, group_rows(i))
        normed = normalize(x, gain1_ref[...])[0].astype(jnp.bfloat16)
        qkv_ref[token_rows(i), :] = dot(normed, wqkv_ref[...]).astype(jnp.bfloat16)

    def attend(i):
        units = []
        for g in range(UNROLL):
            part = pl.ds((i * UNROLL + g) * MEMBERS, MEMBERS)
            for j in range(halves):
                slot = (i * UNROLL + g) * halves + j
                units.append((part, j * LANES, j, pl.ds(slot * MEMBERS, MEMBERS)))
        scores, probs = [], []
        for part, at, j, slot in units:
            q = qkv_ref[part, at : at + LANES]
            k = qkv_ref[part, channels + at : channels + at + LANES]
            q_heads = jnp.concatenate([q] * per, axis=0) * mask_ref[...]
            scores.append(dot(k, q_heads, ((1,), (1,))))
        for (part, at, j, slot), raw in zip(units, scores):
            raw = raw * (scale * LOG2E) + bias_ref[j]
            e = jnp.exp2(raw - jnp.max(raw, axis=0, keepdims=True))
            low = (e * (1.0 / jnp.sum(e, axis=0, keepdims=True))).astype(jnp.bfloat16)
            probs_ref[slot, :] = low
            probs.append(low)
        for (part, at, j, slot), low in zip(units, probs):
            v = qkv_ref[part, 2 * channels + at : 2 * channels + at + LANES]
            context = pick_heads(dot(low, v, ((0,), (0,))), lane_head, per)
            context_ref[part, at : at + LANES] = context.astype(jnp.bfloat16)

    def finish(i):
        rows = group_rows(i)
        x = gather_groups(xs_ref, rows)
        context = context_ref[token_rows(i), :]
        attended = (x + dot(context, wout_ref[...])).astype(jnp.bfloat16).astype(jnp.float32)
        normed2 = normalize(attended, gain2_ref[...])[0].astype(jnp.bfloat16)
        mixed = attended
        wide = wup_ref.shape[1] // 2
        for f in range(2):
            at = slice(f * wide, (f + 1) * wide)
            hidden = gelu(dot(normed2, wup_ref[:, at])).astype(jnp.bfloat16)
            mixed = mixed + dot(hidden, wdown_ref[at, :])
        scatter_groups(mixed_ref, rows, mixed)

    project(0)
    project(1)
    attend(0)
    attend(1)
    finish(0)
    finish(1)
    store_tokens(out_ref, mixed_ref)


def backward_kernel(
    width,
    core_ref,
    data_ref,
    cot_ref,
    qkv_ref,
    probs_ref,
    context_ref,
    gain1_ref,
    wqkv_ref,
    wout_ref,
    out_ref,
    own_ref,
    other_ref,
    acc_ref,
    xs_ref,
    gs_ref,
    grad_ref,
    dctx_ref,
    dqkv_ref,
    mask_ref,
    stage_ref,
    sent,
):
    channels = wout_ref.shape[0]
    halves = channels // LANES
    per = LANES // width
    scale = 1.0 / math.sqrt(width)

    steps = pl.num_programs(1)
    turn = pl.program_id(0) * steps + pl.program_id(1)
    last = pl.num_programs(0) * steps - 1

    @pl.when(turn == 0)
    def _():
        acc_ref[...] = jnp.zeros_like(acc_ref)
        mask_ref[...] = head_mask(mask_ref.shape, width)

    load_tokens(xs_ref, data_ref)
    load_tokens(gs_ref, cot_ref)
    lane_head = lax.broadcasted_iota(jnp.int32, (MEMBERS, LANES), 1) // width

    def project(i):
        here = token_rows(i)
        cot = gather_groups(gs_ref, group_rows(i)).astype(jnp.bfloat16)
        dctx_ref[here, :] = dot(cot, wout_ref[...], ((1,), (1,))).astype(jnp.bfloat16)
        acc_ref[3] += dot(context_ref[here, :], cot, ((0,), (0,)))

    def attend(i):
        units = []
        for g in range(UNROLL):
            part = pl.ds((i * UNROLL + g) * MEMBERS, MEMBERS)
            for j in range(halves):
                slot = (i * UNROLL + g) * halves + j
                units.append((part, j * LANES, pl.ds(slot * MEMBERS, MEMBERS)))

        def put(n, part, at, value):
            to = n * channels + at
            dqkv_ref[part, to : to + LANES] = value.astype(jnp.bfloat16)

        d_probs, d_scaled = [], []
        for part, at, slot in units:
            v = qkv_ref[part, 2 * channels + at : 2 * channels + at + LANES]
            dc_heads = jnp.concatenate([dctx_ref[part, at : at + LANES]] * per, axis=0) * mask_ref[...]
            d_probs.append(dot(v, dc_heads, ((1,), (1,))))
            put(2, part, at, dot(probs_ref[slot, :], dc_heads))
        for (part, at, slot), dp in zip(units, d_probs):
            probs = probs_ref[slot, :].astype(jnp.float32)
            delta = jnp.sum(probs * dp, axis=0, keepdims=True)
            delta = delta / jnp.sum(probs, axis=0, keepdims=True)
            d_scaled.append((probs * (dp - delta) * scale).astype(jnp.bfloat16))
        for (part, at, slot), ds in zip(units, d_scaled):
            q_heads = jnp.concatenate([qkv_ref[part, at : at + LANES]] * per, axis=0) * mask_ref[...]
            put(1, part, at, dot(ds, q_heads))
            k = qkv_ref[part, channels + at : channels + at + LANES]
            put(0, part, at, pick_heads(dot(ds, k, ((0,), (0,))), lane_head, per))

    def finish(i):
        rows = group_rows(i)
        x = gather_groups(xs_ref, rows)
        d_qkv = dqkv_ref[token_rows(i), :]
        normed_wide, unit, inverse = normalize(x, gain1_ref[...])
        d_weight = dot(normed_wide.astype(jnp.bfloat16), d_qkv, ((0,), (0,)))
        for n in range(3):
            acc_ref[n] += d_weight[:, n * channels : (n + 1) * channels]
        d_unit = dot(d_qkv, wqkv_ref[...], ((1,), (1,))) * gain1_ref[...]
        grad = gather_groups(gs_ref, rows) + inverse * (
            d_unit
            - jnp.mean(d_unit, axis=-1, keepdims=True)
            - unit * jnp.mean(d_unit * unit, axis=-1, keepdims=True)
        )
        scatter_groups(grad_ref, rows, grad)

    project(0)
    project(1)
    attend(0)
    attend(1)
    finish(0)
    finish(1)

    def send(n):
        rows = pl.ds(n % steps * BLOCK, BLOCK)
        return pltpu.make_async_copy(
            stage_ref.at[n % 2], out_ref.at[:, n // steps, :, rows, :], sent.at[n % 2]
        )

    @pl.when(turn >= 2)
    def _():
        send(turn - 2).wait()

    for j in range(halves):
        wide = grad_ref[j].reshape(GRID, GRID, BLOCK, LANES)
        stage_ref[turn % 2, :, :, :, j * LANES : (j + 1) * LANES] = wide.astype(jnp.bfloat16)
    send(turn).start()

    @pl.when(turn == last)
    def _():
        count = own_ref.shape[0] // GRID
        halved = acc_ref[...].reshape(GRID, CORES, count, channels)
        first, second = (halved[:, c].reshape(own_ref.shape) for c in range(CORES))

        @pl.when(core_ref[0] == 0)
        def _():
            own_ref[...] = first
            other_ref[...] = second

        @pl.when(core_ref[0] == 1)
        def _():
            own_ref[...] = second
            other_ref[...] = first

        send(turn - 1).wait()
        send(turn).wait()


def specs(data):
    _, classes, _, positions, channels = data.shape
    steps = positions // BLOCK
    grid = (classes, steps)
    block = pl.BlockSpec((GRID, 1, GRID, BLOCK, channels), lambda c, p: (0, c, 0, p, 0))
    whole = lambda a: pl.BlockSpec(a.shape, lambda c, p: (0,) * a.ndim)
    flat = lambda rows, width: pl.BlockSpec((rows, width), lambda c, p: (c * steps + p, 0))
    return grid, block, whole, flat, classes * positions


PARAMS = pltpu.CompilerParams(vmem_limit_bytes=VMEM_LIMIT)


def forward(data, gain1, wqkv, wout, pos_bias, gain2, wup, wdown, width):
    grid, block, whole, flat, groups = specs(data)
    channels = data.shape[-1]
    halves = channels // LANES
    tokens = MEMBERS * BLOCK
    count = groups * MEMBERS
    ff = wup.shape[1]
    row_width = LANES // width * MEMBERS
    weights = (gain1, wqkv, wout, pos_bias, gain2, wup, wdown)
    return pl.pallas_call(
        functools.partial(forward_kernel, width),
        grid=grid,
        in_specs=[block] + [whole(a) for a in weights],
        out_specs=[
            block,
            flat(tokens, 3 * channels),
            flat(tokens * halves, row_width),
            flat(tokens, channels),
        ],
        out_shape=[
            pltpu.VMEM(data.shape, jnp.bfloat16),
            pltpu.HBM((count, 3 * channels), jnp.bfloat16),
            pltpu.HBM((count * halves, row_width), jnp.bfloat16),
            pltpu.HBM((count, channels), jnp.bfloat16),
        ],
        scratch_shapes=[pltpu.VMEM((halves, tokens, LANES), jnp.float32)] * 2
        + [
            pltpu.VMEM((row_width, LANES), jnp.bfloat16),
            pltpu.VMEM((halves, MEMBERS, row_width), jnp.float32),
        ],
        compiler_params=PARAMS,
        cost_estimate=pl.CostEstimate(
            flops=count * 2 * channels * (16 * channels + 2 * ff),
            bytes_accessed=2 * count * channels * 8,
            transcendentals=count * ff,
        ),
    )(data, *weights)


def backward(core, data, cot, qkv, probs, context, gain1, wqkv, wout, width):
    grid, block, whole, flat, groups = specs(data)
    channels = data.shape[-1]
    halves = channels // LANES
    tokens = MEMBERS * BLOCK
    count = groups * MEMBERS
    row_width = LANES // width * MEMBERS
    rows = data.shape[3] + 4 * channels // (GRID * CORES * GRID)
    pieces = (4 * channels // CORES, channels)
    qkv, probs, context = (
        pltpu.with_memory_space_constraint(a, pltpu.HBM) for a in (qkv, probs, context)
    )
    cot = pltpu.with_memory_space_constraint(cot, pltpu.HBM)
    weights = (gain1, wqkv, wout)
    return pl.pallas_call(
        functools.partial(backward_kernel, width),
        grid=grid,
        in_specs=[
            pl.BlockSpec(memory_space=pltpu.SMEM),
            block,
            block,
            flat(tokens, 3 * channels),
            flat(tokens * halves, row_width),
            flat(tokens, channels),
        ]
        + [whole(a) for a in weights],
        out_specs=[
            pl.BlockSpec(memory_space=pl.ANY),
            pl.BlockSpec(pieces, lambda c, p: (0, 0)),
            pl.BlockSpec(pieces, lambda c, p: (0, 0)),
        ],
        out_shape=[
            pltpu.VMEM(data.shape[:3] + (rows, channels), jnp.bfloat16),
            jax.ShapeDtypeStruct(pieces, jnp.float32),
            jax.ShapeDtypeStruct(pieces, jnp.float32),
        ],
        scratch_shapes=[pltpu.VMEM((4, channels, channels), jnp.float32)]
        + [pltpu.VMEM((halves, tokens, LANES), jnp.float32)] * 3
        + [
            pltpu.VMEM((tokens, channels), jnp.bfloat16),
            pltpu.VMEM((tokens, 3 * channels), jnp.bfloat16),
            pltpu.VMEM((row_width, LANES), jnp.bfloat16),
            pltpu.VMEM((2, GRID, GRID, BLOCK, channels), jnp.bfloat16),
            pltpu.SemaphoreType.DMA((2,)),
        ],
        compiler_params=PARAMS,
        cost_estimate=pl.CostEstimate(
            flops=count * 2 * channels * 24 * channels,
            bytes_accessed=2 * count * channels * 10,
            transcendentals=0,
        ),
    )(core, data, cot, qkv, probs, context, *weights)


def place_kernel(source_ref, out_ref):
    out_ref[...] = source_ref[...]


def placed(values, space=None):
    rows, columns, channels = values.shape
    block = pl.BlockSpec((rows // 4, columns, channels), lambda i: (i, 0, 0))
    return pl.pallas_call(
        place_kernel,
        grid=(4,),
        in_specs=[block],
        out_specs=block,
        out_shape=(space or jax.ShapeDtypeStruct)(values.shape, values.dtype),
        cost_estimate=pl.CostEstimate(
            flops=0, bytes_accessed=4 * values.size, transcendentals=0
        ),
    )(values)


def trim_kernel(source_ref, out_ref):
    rows, columns, channels = out_ref.shape
    positions = rows * columns // source_ref.shape[0]
    out_ref[...] = source_ref[:, :positions, :].reshape(out_ref.shape)


def trimmed(values, shape):
    rows, columns, channels = shape
    devices, height, _ = values.shape
    return pl.pallas_call(
        trim_kernel,
        grid=(4,),
        in_specs=[pl.BlockSpec((devices // 4, height, channels), lambda i: (i, 0, 0))],
        out_specs=pl.BlockSpec((rows // 4, columns, channels), lambda i: (i, 0, 0)),
        out_shape=jax.ShapeDtypeStruct(shape, values.dtype),
        compiler_params=pltpu.CompilerParams(vmem_limit_bytes=16 * 1024 * 1024),
        cost_estimate=pl.CostEstimate(
            flops=0, bytes_accessed=4 * values.size, transcendentals=0
        ),
    )(values)


def local(tokens, cotangent, norm1_gain, w_qkv, w_out, pos_bias, norm2_gain, w_up, w_down):
    tile_rows, tile_cols, channels = tokens.shape
    columns = lax.axis_size("gx")
    devices = lax.axis_size(AXES)
    core = lax.axis_index("gy") % CORES
    positions = tile_rows * tile_cols // MEMBERS
    factor = 1.0 / math.sqrt(tile_rows * tile_cols * devices)
    width = channels // pos_bias.shape[0]
    gain1, gain2 = norm1_gain.reshape(1, -1), norm2_gain.reshape(1, -1)
    sent = (MEMBERS, positions, channels)
    kept = (GRID, 1, GRID, positions, channels)
    def device(row, c, column):
        return (row * CORES + c) * columns + column

    members = [(row, column) for row in range(GRID) for column in range(GRID)]
    peers = [[device(row, c, column) for row, column in members] for c in range(CORES)]
    partner = [
        (device(row, c, column), device(row, 1 - c, column))
        for row, column in members
        for c in range(CORES)
    ]

    def exchange(pieces):
        return lax.all_to_all(pieces, AXES, 0, 0, axis_index_groups=peers, tiled=True)

    data = exchange(tokens.reshape(sent)).reshape(kept)
    cot = exchange(placed(cotangent, pltpu.VMEM).reshape(sent)).reshape(kept)
    mixed, qkv, probs, context = forward(
        data, gain1, w_qkv, w_out, pos_bias, gain2, w_up, w_down, width
    )
    mixed = exchange(mixed.reshape(sent)).reshape(tokens.shape)
    grad, own_pieces, other_pieces = backward(
        core.reshape(1), data, cot, qkv, probs, context, gain1, w_qkv, w_out, width
    )
    pair = own_pieces + lax.ppermute(other_pieces, AXES, partner)
    pair = pair.astype(jnp.bfloat16).reshape(GRID, 1, GRID, -1, channels)
    grad = lax.dynamic_update_slice(grad, pair, (0, 0, 0, positions, 0))
    grad, mixed = lax.optimization_barrier((grad.reshape(MEMBERS, -1, channels), mixed))
    grad = exchange(grad)
    total = jnp.sum(grad[:, positions:].astype(jnp.float32), axis=0) * factor
    total = jnp.broadcast_to(total.astype(jnp.bfloat16)[None], (devices,) + total.shape)
    total = lax.all_to_all(total, AXES, 0, 0, tiled=True)
    blocks = total.astype(jnp.float32).reshape(4, channels, channels)
    grad_qkv = jnp.concatenate([blocks[0], blocks[1], blocks[2]], axis=1)
    grad, mixed = lax.optimization_barrier((trimmed(grad, tokens.shape), mixed))
    return (placed(mixed), grad, grad_qkv, blocks[3])


def solution(mesh):
    placed = (P("gy", "gx", None), P("gy", "gx", None), P(), P(), P(), P(), P(), P(), P())
    return jax.shard_map(
        local,
        mesh=mesh,
        in_specs=placed,
        out_specs=(P("gy", "gx", None), P("gy", "gx", None), P(), P()),
        check_vma=False,
    )
```

```python
import functools
import math

import jax
import jax.numpy as jnp
from jax import lax
from jax.experimental import pallas as pl
from jax.experimental.pallas import tpu as pltpu
from jax.sharding import PartitionSpec as P

GRID = 8
CORES = 2
MEMBERS = GRID * GRID
EPSILON = 1e-05
LOG2E = math.log2(math.e)
AXES = ("gy", "gx")
LANES = 128
BLOCK = 16
DENSE = 8
UNROLL = 8
VMEM_LIMIT = 36 * 1024 * 1024


def dot(a, b, contract=((1,), (0,))):
    return lax.dot_general(a, b, (contract, ((), ())), preferred_element_type=jnp.float32)


def normalize(wide, gain):
    centre = jnp.mean(wide, axis=-1, keepdims=True)
    shifted = wide - centre
    variance = jnp.mean(shifted * shifted, axis=-1, keepdims=True)
    inverse = lax.rsqrt(variance + EPSILON)
    unit = shifted * inverse
    return unit * gain, unit, inverse


def gelu(x):
    inner = x * (0.7978845608028654 + 0.035677408136300125 * (x * x))
    half = 0.5 * x
    return half + half * jnp.tanh(inner)


def pick_heads(full, lane_head, per):
    out = full[(per - 1) * MEMBERS : per * MEMBERS]
    for h in range(per - 2, -1, -1):
        out = jnp.where(lane_head == h, full[h * MEMBERS : (h + 1) * MEMBERS], out)
    return out


def load_tokens(scratch_ref, data_ref):
    halves, tokens, _ = scratch_ref.shape
    for j in range(halves):
        lanes = slice(j * LANES, (j + 1) * LANES)
        scratch_ref[j] = data_ref[:, 0, :, :, lanes].reshape(tokens, LANES).astype(jnp.float32)


def store_tokens(data_ref, scratch_ref):
    halves = scratch_ref.shape[0]
    for j in range(halves):
        lanes = slice(j * LANES, (j + 1) * LANES)
        wide = scratch_ref[j].reshape(GRID, GRID, BLOCK, LANES)
        data_ref[:, 0, :, :, lanes] = wide.astype(jnp.bfloat16)


def head_mask(shape, width):
    row_head = lax.broadcasted_iota(jnp.int32, shape, 0) // MEMBERS
    lane_head = lax.broadcasted_iota(jnp.int32, shape, 1) // width
    return (row_head == lane_head).astype(jnp.float32).astype(jnp.bfloat16)


def group_rows(i):
    return [pl.ds(i * DENSE + g, MEMBERS, stride=BLOCK) for g in range(DENSE)]


def token_rows(i):
    count = DENSE * MEMBERS
    return pl.ds(i * count, count)


def gather_groups(ref, rows):
    halves = ref.shape[0]
    return jnp.concatenate(
        [jnp.concatenate([ref[j, r, :] for j in range(halves)], axis=1) for r in rows], axis=0
    )


def scatter_groups(ref, rows, values):
    for g, r in enumerate(rows):
        for j in range(ref.shape[0]):
            ref[j, r, :] = values[g * MEMBERS : (g + 1) * MEMBERS, j * LANES : (j + 1) * LANES]


def repeat(count, step):
    for i in range(count):
        step(i)


def forward_kernel(
    width,
    data_ref,
    gain1_ref,
    wqkv_ref,
    wout_ref,
    pos_ref,
    gain2_ref,
    wup_ref,
    wdown_ref,
    out_ref,
    qkv_ref,
    probs_ref,
    context_ref,
    xs_ref,
    mixed_ref,
    mask_ref,
    bias_ref,
):
    channels = wout_ref.shape[0]
    halves = channels // LANES
    per = LANES // width
    scale = 1.0 / math.sqrt(width)
    @pl.when((pl.program_id(0) == 0) & (pl.program_id(1) == 0))
    def _():
        mask_ref[...] = head_mask(mask_ref.shape, width)
        for j in range(halves):
            for h in range(per):
                lanes = slice(h * MEMBERS, (h + 1) * MEMBERS)
                bias_ref[j, :, lanes] = pos_ref[j * per + h].T * LOG2E

    load_tokens(xs_ref, data_ref)
    lane_head = lax.broadcasted_iota(jnp.int32, (MEMBERS, LANES), 1) // width

    def project(i):
        x = gather_groups(xs_ref, group_rows(i))
        normed = normalize(x, gain1_ref[...])[0].astype(jnp.bfloat16)
        qkv_ref[token_rows(i), :] = dot(normed, wqkv_ref[...]).astype(jnp.bfloat16)

    def attend(i):
        units = []
        for g in range(UNROLL):
            part = pl.ds((i * UNROLL + g) * MEMBERS, MEMBERS)
            for j in range(halves):
                slot = (i * UNROLL + g) * halves + j
                units.append((part, j * LANES, j, pl.ds(slot * MEMBERS, MEMBERS)))
        scores, probs = [], []
        for part, at, j, slot in units:
            q = qkv_ref[part, at : at + LANES]
            k = qkv_ref[part, channels + at : channels + at + LANES]
            q_heads = jnp.concatenate([q] * per, axis=0) * mask_ref[...]
            scores.append(dot(k, q_heads, ((1,), (1,))))
        for (part, at, j, slot), raw in zip(units, scores):
            raw = raw * (scale * LOG2E) + bias_ref[j]
            e = jnp.exp2(raw - jnp.max(raw, axis=0, keepdims=True))
            low = (e * (1.0 / jnp.sum(e, axis=0, keepdims=True))).astype(jnp.bfloat16)
            probs_ref[slot, :] = low
            probs.append(low)
        for (part, at, j, slot), low in zip(units, probs):
            v = qkv_ref[part, 2 * channels + at : 2 * channels + at + LANES]
            context = pick_heads(dot(low, v, ((0,), (0,))), lane_head, per)
            context_ref[part, at : at + LANES] = context.astype(jnp.bfloat16)

    def finish(i):
        rows = group_rows(i)
        x = gather_groups(xs_ref, rows)
        context = context_ref[token_rows(i), :]
        attended = (x + dot(context, wout_ref[...])).astype(jnp.bfloat16).astype(jnp.float32)
        normed2 = normalize(attended, gain2_ref[...])[0].astype(jnp.bfloat16)
        mixed = attended
        wide = wup_ref.shape[1] // 2
        for f in range(2):
            at = slice(f * wide, (f + 1) * wide)
            hidden = gelu(dot(normed2, wup_ref[:, at])).astype(jnp.bfloat16)
            mixed = mixed + dot(hidden, wdown_ref[at, :])
        scatter_groups(mixed_ref, rows, mixed)

    project(0)
    project(1)
    attend(0)
    attend(1)
    finish(0)
    finish(1)
    store_tokens(out_ref, mixed_ref)


def backward_kernel(
    width,
    core_ref,
    data_ref,
    cot_ref,
    qkv_ref,
    probs_ref,
    context_ref,
    gain1_ref,
    wqkv_ref,
    wout_ref,
    out_ref,
    own_ref,
    other_ref,
    acc_ref,
    xs_ref,
    gs_ref,
    grad_ref,
    dctx_ref,
    dqkv_ref,
    mask_ref,
    stage_ref,
    sent,
):
    channels = wout_ref.shape[0]
    halves = channels // LANES
    per = LANES // width
    scale = 1.0 / math.sqrt(width)

    steps = pl.num_programs(1)
    turn = pl.program_id(0) * steps + pl.program_id(1)
    last = pl.num_programs(0) * steps - 1

    @pl.when(turn == 0)
    def _():
        acc_ref[...] = jnp.zeros_like(acc_ref)
        mask_ref[...] = head_mask(mask_ref.shape, width)

    load_tokens(xs_ref, data_ref)
    load_tokens(gs_ref, cot_ref)
    lane_head = lax.broadcasted_iota(jnp.int32, (MEMBERS, LANES), 1) // width

    def project(i):
        here = token_rows(i)
        cot = gather_groups(gs_ref, group_rows(i)).astype(jnp.bfloat16)
        dctx_ref[here, :] = dot(cot, wout_ref[...], ((1,), (1,))).astype(jnp.bfloat16)
        acc_ref[3] += dot(context_ref[here, :], cot, ((0,), (0,)))

    def attend(i):
        units = []
        for g in range(UNROLL):
            part = pl.ds((i * UNROLL + g) * MEMBERS, MEMBERS)
            for j in range(halves):
                slot = (i * UNROLL + g) * halves + j
                units.append((part, j * LANES, pl.ds(slot * MEMBERS, MEMBERS)))

        def put(n, part, at, value):
            to = n * channels + at
            dqkv_ref[part, to : to + LANES] = value.astype(jnp.bfloat16)

        d_probs, d_scaled = [], []
        for part, at, slot in units:
            v = qkv_ref[part, 2 * channels + at : 2 * channels + at + LANES]
            dc_heads = jnp.concatenate([dctx_ref[part, at : at + LANES]] * per, axis=0) * mask_ref[...]
            d_probs.append(dot(v, dc_heads, ((1,), (1,))))
            put(2, part, at, dot(probs_ref[slot, :], dc_heads))
        for (part, at, slot), dp in zip(units, d_probs):
            probs = probs_ref[slot, :].astype(jnp.float32)
            delta = jnp.sum(probs * dp, axis=0, keepdims=True)
            delta = delta / jnp.sum(probs, axis=0, keepdims=True)
            d_scaled.append((probs * (dp - delta) * scale).astype(jnp.bfloat16))
        for (part, at, slot), ds in zip(units, d_scaled):
            q_heads = jnp.concatenate([qkv_ref[part, at : at + LANES]] * per, axis=0) * mask_ref[...]
            put(1, part, at, dot(ds, q_heads))
            k = qkv_ref[part, channels + at : channels + at + LANES]
            put(0, part, at, pick_heads(dot(ds, k, ((0,), (0,))), lane_head, per))

    def finish(i):
        rows = group_rows(i)
        x = gather_groups(xs_ref, rows)
        d_qkv = dqkv_ref[token_rows(i), :]
        normed_wide, unit, inverse = normalize(x, gain1_ref[...])
        d_weight = dot(normed_wide.astype(jnp.bfloat16), d_qkv, ((0,), (0,)))
        for n in range(3):
            acc_ref[n] += d_weight[:, n * channels : (n + 1) * channels]
        d_unit = dot(d_qkv, wqkv_ref[...], ((1,), (1,))) * gain1_ref[...]
        grad = gather_groups(gs_ref, rows) + inverse * (
            d_unit
            - jnp.mean(d_unit, axis=-1, keepdims=True)
            - unit * jnp.mean(d_unit * unit, axis=-1, keepdims=True)
        )
        scatter_groups(grad_ref, rows, grad)

    project(0)
    project(1)
    attend(0)
    attend(1)
    finish(0)
    finish(1)

    def send(n):
        rows = pl.ds(n % steps * BLOCK, BLOCK)
        return pltpu.make_async_copy(
            stage_ref.at[n % 2], out_ref.at[:, n // steps, :, rows, :], sent.at[n % 2]
        )

    @pl.when(turn >= 2)
    def _():
        send(turn - 2).wait()

    for j in range(halves):
        wide = grad_ref[j].reshape(GRID, GRID, BLOCK, LANES)
        stage_ref[turn % 2, :, :, :, j * LANES : (j + 1) * LANES] = wide.astype(jnp.bfloat16)
    send(turn).start()

    @pl.when(turn == last)
    def _():
        count = own_ref.shape[0] // GRID
        halved = acc_ref[...].reshape(GRID, CORES, count, channels)
        first, second = (halved[:, c].reshape(own_ref.shape) for c in range(CORES))

        @pl.when(core_ref[0] == 0)
        def _():
            own_ref[...] = first
            other_ref[...] = second

        @pl.when(core_ref[0] == 1)
        def _():
            own_ref[...] = second
            other_ref[...] = first

        send(turn - 1).wait()
        send(turn).wait()


def specs(data):
    _, classes, _, positions, channels = data.shape
    steps = positions // BLOCK
    grid = (classes, steps)
    block = pl.BlockSpec((GRID, 1, GRID, BLOCK, channels), lambda c, p: (0, c, 0, p, 0))
    whole = lambda a: pl.BlockSpec(a.shape, lambda c, p: (0,) * a.ndim)
    flat = lambda rows, width: pl.BlockSpec((rows, width), lambda c, p: (c * steps + p, 0))
    return grid, block, whole, flat, classes * positions


PARAMS = pltpu.CompilerParams(vmem_limit_bytes=VMEM_LIMIT)


def forward(data, gain1, wqkv, wout, pos_bias, gain2, wup, wdown, width):
    grid, block, whole, flat, groups = specs(data)
    channels = data.shape[-1]
    halves = channels // LANES
    tokens = MEMBERS * BLOCK
    count = groups * MEMBERS
    ff = wup.shape[1]
    row_width = LANES // width * MEMBERS
    weights = (gain1, wqkv, wout, pos_bias, gain2, wup, wdown)
    return pl.pallas_call(
        functools.partial(forward_kernel, width),
        grid=grid,
        in_specs=[block] + [whole(a) for a in weights],
        out_specs=[
            block,
            flat(tokens, 3 * channels),
            flat(tokens * halves, row_width),
            flat(tokens, channels),
        ],
        out_shape=[
            pltpu.VMEM(data.shape, jnp.bfloat16),
            pltpu.HBM((count, 3 * channels), jnp.bfloat16),
            pltpu.HBM((count * halves, row_width), jnp.bfloat16),
            pltpu.HBM((count, channels), jnp.bfloat16),
        ],
        scratch_shapes=[pltpu.VMEM((halves, tokens, LANES), jnp.float32)] * 2
        + [
            pltpu.VMEM((row_width, LANES), jnp.bfloat16),
            pltpu.VMEM((halves, MEMBERS, row_width), jnp.float32),
        ],
        compiler_params=PARAMS,
        cost_estimate=pl.CostEstimate(
            flops=count * 2 * channels * (16 * channels + 2 * ff),
            bytes_accessed=2 * count * channels * 8,
            transcendentals=count * ff,
        ),
    )(data, *weights)


def backward(core, data, cot, qkv, probs, context, gain1, wqkv, wout, width):
    grid, block, whole, flat, groups = specs(data)
    channels = data.shape[-1]
    halves = channels // LANES
    tokens = MEMBERS * BLOCK
    count = groups * MEMBERS
    row_width = LANES // width * MEMBERS
    rows = data.shape[3]
    pieces = (4 * channels // CORES, channels)
    qkv, probs, context = (
        pltpu.with_memory_space_constraint(a, pltpu.HBM) for a in (qkv, probs, context)
    )
    cot = pltpu.with_memory_space_constraint(cot, pltpu.HBM)
    weights = (gain1, wqkv, wout)
    return pl.pallas_call(
        functools.partial(backward_kernel, width),
        grid=grid,
        in_specs=[
            pl.BlockSpec(memory_space=pltpu.SMEM),
            block,
            block,
            flat(tokens, 3 * channels),
            flat(tokens * halves, row_width),
            flat(tokens, channels),
        ]
        + [whole(a) for a in weights],
        out_specs=[
            pl.BlockSpec(memory_space=pl.ANY),
            pl.BlockSpec(pieces, lambda c, p: (0, 0)),
            pl.BlockSpec(pieces, lambda c, p: (0, 0)),
        ],
        out_shape=[
            pltpu.VMEM(data.shape[:3] + (rows, channels), jnp.bfloat16),
            jax.ShapeDtypeStruct(pieces, jnp.float32),
            jax.ShapeDtypeStruct(pieces, jnp.float32),
        ],
        scratch_shapes=[pltpu.VMEM((4, channels, channels), jnp.float32)]
        + [pltpu.VMEM((halves, tokens, LANES), jnp.float32)] * 3
        + [
            pltpu.VMEM((tokens, channels), jnp.bfloat16),
            pltpu.VMEM((tokens, 3 * channels), jnp.bfloat16),
            pltpu.VMEM((row_width, LANES), jnp.bfloat16),
            pltpu.VMEM((2, GRID, GRID, BLOCK, channels), jnp.bfloat16),
            pltpu.SemaphoreType.DMA((2,)),
        ],
        compiler_params=PARAMS,
        cost_estimate=pl.CostEstimate(
            flops=count * 2 * channels * 24 * channels,
            bytes_accessed=2 * count * channels * 10,
            transcendentals=0,
        ),
    )(core, data, cot, qkv, probs, context, *weights)


def place_kernel(source_ref, out_ref):
    out_ref[...] = source_ref[...]


def placed(values, space=None):
    rows, columns, channels = values.shape
    block = pl.BlockSpec((rows // 4, columns, channels), lambda i: (i, 0, 0))
    return pl.pallas_call(
        place_kernel,
        grid=(4,),
        in_specs=[block],
        out_specs=block,
        out_shape=(space or jax.ShapeDtypeStruct)(values.shape, values.dtype),
        cost_estimate=pl.CostEstimate(
            flops=0, bytes_accessed=4 * values.size, transcendentals=0
        ),
    )(values)


def join_kernel(grad_ref, own_ref, other_ref, out_ref):
    positions = grad_ref.shape[1]
    pair = (own_ref[...] + other_ref[...]).astype(jnp.bfloat16)
    out_ref[:, :positions, :] = grad_ref[...]
    out_ref[:, positions:, :] = pair.reshape(out_ref.shape[0], -1, out_ref.shape[2])


def joined(grad, own, other):
    peers, positions, channels = grad.shape
    height = positions + own.shape[0] // peers
    piece = pl.BlockSpec((own.shape[0] // 4, channels), lambda i: (i, 0))
    return pl.pallas_call(
        join_kernel,
        grid=(4,),
        in_specs=[
            pl.BlockSpec((peers // 4, positions, channels), lambda i: (i, 0, 0)),
            piece,
            piece,
        ],
        out_specs=pl.BlockSpec((peers // 4, height, channels), lambda i: (i, 0, 0)),
        out_shape=pltpu.VMEM((peers, height, channels), grad.dtype),
        compiler_params=pltpu.CompilerParams(vmem_limit_bytes=16 * 1024 * 1024),
        cost_estimate=pl.CostEstimate(
            flops=own.size, bytes_accessed=4 * grad.size, transcendentals=0
        ),
    )(grad, own, other)


def trim_kernel(source_ref, out_ref):
    rows, columns, channels = out_ref.shape
    positions = rows * columns // source_ref.shape[0]
    out_ref[...] = source_ref[:, :positions, :].reshape(out_ref.shape)


def trimmed(values, shape):
    rows, columns, channels = shape
    devices, height, _ = values.shape
    return pl.pallas_call(
        trim_kernel,
        grid=(4,),
        in_specs=[pl.BlockSpec((devices // 4, height, channels), lambda i: (i, 0, 0))],
        out_specs=pl.BlockSpec((rows // 4, columns, channels), lambda i: (i, 0, 0)),
        out_shape=jax.ShapeDtypeStruct(shape, values.dtype),
        compiler_params=pltpu.CompilerParams(vmem_limit_bytes=16 * 1024 * 1024),
        cost_estimate=pl.CostEstimate(
            flops=0, bytes_accessed=4 * values.size, transcendentals=0
        ),
    )(values)


def local(tokens, cotangent, norm1_gain, w_qkv, w_out, pos_bias, norm2_gain, w_up, w_down):
    tile_rows, tile_cols, channels = tokens.shape
    columns = lax.axis_size("gx")
    devices = lax.axis_size(AXES)
    core = lax.axis_index("gy") % CORES
    positions = tile_rows * tile_cols // MEMBERS
    factor = 1.0 / math.sqrt(tile_rows * tile_cols * devices)
    width = channels // pos_bias.shape[0]
    gain1, gain2 = norm1_gain.reshape(1, -1), norm2_gain.reshape(1, -1)
    sent = (MEMBERS, positions, channels)
    kept = (GRID, 1, GRID, positions, channels)
    def device(row, c, column):
        return (row * CORES + c) * columns + column

    members = [(row, column) for row in range(GRID) for column in range(GRID)]
    peers = [[device(row, c, column) for row, column in members] for c in range(CORES)]
    partner = [
        (device(row, c, column), device(row, 1 - c, column))
        for row, column in members
        for c in range(CORES)
    ]

    def exchange(pieces):
        return lax.all_to_all(pieces, AXES, 0, 0, axis_index_groups=peers, tiled=True)

    data = exchange(tokens.reshape(sent)).reshape(kept)
    cot = exchange(placed(cotangent, pltpu.VMEM).reshape(sent)).reshape(kept)
    mixed, qkv, probs, context = forward(
        data, gain1, w_qkv, w_out, pos_bias, gain2, w_up, w_down, width
    )
    mixed = exchange(mixed.reshape(sent)).reshape(tokens.shape)
    grad, own_pieces, other_pieces = backward(
        core.reshape(1), data, cot, qkv, probs, context, gain1, w_qkv, w_out, width
    )
    other_pieces = lax.ppermute(other_pieces, AXES, partner)
    grad = joined(grad.reshape(sent), own_pieces, other_pieces)
    grad, mixed = lax.optimization_barrier((grad, mixed))
    grad = exchange(grad)
    total = jnp.sum(grad[:, positions:].astype(jnp.float32), axis=0) * factor
    total = jnp.broadcast_to(total.astype(jnp.bfloat16)[None], (devices,) + total.shape)
    total = lax.all_to_all(total, AXES, 0, 0, tiled=True)
    blocks = total.astype(jnp.float32).reshape(4, channels, channels)
    grad_qkv = jnp.concatenate([blocks[0], blocks[1], blocks[2]], axis=1)
    grad, mixed = lax.optimization_barrier((trimmed(grad, tokens.shape), mixed))
    return (placed(mixed), grad, grad_qkv, blocks[3])


def solution(mesh):
    placed = (P("gy", "gx", None), P("gy", "gx", None), P(), P(), P(), P(), P(), P(), P())
    return jax.shard_map(
        local,
        mesh=mesh,
        in_specs=placed,
        out_specs=(P("gy", "gx", None), P("gy", "gx", None), P(), P()),
        check_vma=False,
    )
```
